256 devices in a mesh: dp: 16 (over y, x), shard: 16 (over z, core).
Axes of the slice: x: 4, y: 4, z: 8, core: 2. Of those that a mesh axis runs over, the one named last changes fastest.
Arguments:
- features: bfloat16 [131072, 128], P('dp'), may hold values from -160 to 160
- anchors: float32 [2048, 128], P('shard'), may hold values from -6 to 6
- metric: float32 [4, 128], replicated, may hold values from 0.5 to 1.5
- classifier: float32 [128, 172], replicated, may hold values from -0.5 to 0.5
- labels: int32 [131072], P('dp'), may hold values from 0 to 171
- train_mask: int32 [131072], P('dp'), may hold values 0 or 1
Outputs:
- embedding: bfloat16 [131072, 128], P(('dp', 'shard'))
- loss: float32 [], replicated
- grad_classifier: float32 [128, 172], replicated
- grad_anchors: float32 [2048, 128], P('shard')
- grad_metric: float32 [4, 128], replicated
The draws below stay inside these ranges and needn't reach their ends.
All inputs are finite; a program needn't handle non-finite values. No bound on the sum of `train_mask` on one device may be relied on, other than what follows from the above.
Results may differ from the reference program's by a relative error of at most 0.009.
Values may be sent and summed in bfloat16 or wider, within the bound.
No kernel may reach another device: no remote copies, remote signals or barrier semaphores. Data moves between devices by JAX's collectives and lax.ppermute only.
A program may use at most 128 MiB of HBM per device.

```python
import jax
import jax.numpy as jnp
from jax import lax

F = 128
HEADS = 4
CLASSES = 172
ROWS_DEV = 8192
ANCHORS = 2048
NODES = 131072
N_DP = 16


def anchor_matrix(key):
    base_key = jax.random.fold_in(key, 101)
    matrix = jnp.clip(jax.random.normal(base_key, (ANCHORS, F), jnp.float32), -6.0, 6.0)
    return matrix


def draw_anchors(key, part):
    return anchor_matrix(key)


def draw_features(key, part):
    matrix = anchor_matrix(key)
    first_pick = jax.random.randint(jax.random.fold_in(key, 102), (NODES,), 0, ANCHORS - ANCHORS // 8)
    second_pick = jax.random.randint(jax.random.fold_in(key, 103), (NODES,), 0, ANCHORS - ANCHORS // 8)
    node_kind = jax.random.randint(jax.random.fold_in(key, 104), (NODES,), 0, 5)
    weights = jax.random.uniform(jax.random.fold_in(key, 105), (NODES, 2), jnp.float32, 0.5, 1.0)
    noise_part = 0.6 * jax.random.normal(jax.random.fold_in(key, 106), (NODES, F), jnp.float32)
    mixture = weights[:, 0:1] * matrix[first_pick] + weights[:, 1:2] * matrix[second_pick]
    live_rows = (node_kind > 0).astype(jnp.float32)[:, None]
    return jnp.clip(live_rows * mixture + noise_part, -160.0, 160.0).astype(jnp.bfloat16)


def set_ends(values, stream_key, least, largest):
    longest = values.shape.index(max(values.shape))
    spots = []
    for shift in (0, 1):
        where = [jax.random.randint(jax.random.fold_in(stream_key, axis), (), 0, length) for axis, length in enumerate(values.shape)]
        where[longest] = (where[longest] + shift) % values.shape[longest]
        spots.append(tuple(where))
    return values.at[spots[0]].set(least).at[spots[1]].set(largest)


def bell_draw(rng, shape, deviation, most, kind=jnp.bfloat16):
    array = deviation * jax.random.normal(rng, shape, jnp.float32)
    return jnp.clip(array, min=-most, max=most).astype(kind)


def setup_inputs(seed: int = 0) -> dict:
    key_list = jax.random.split(jax.random.key(seed), 7)
    return {
        "features": draw_features(jax.random.fold_in(key_list[6], 71), 0),
        "anchors": draw_anchors(jax.random.fold_in(key_list[6], 71), 0),
        "metric": jnp.clip(jax.random.uniform(key_list[2], (HEADS, F), jnp.float32, 0.5, 1.5), 0.5, 1.5),
        "classifier": bell_draw(key_list[3], (F, CLASSES), F ** -0.5, 0.5, jnp.float32),
        "labels": set_ends(jax.random.randint(key_list[4], (NODES,), 0, CLASSES), jax.random.fold_in(key_list[4], 1), 0, CLASSES - 1).astype(jnp.int32),
        "train_mask": set_ends((jax.random.randint(key_list[5], (NODES,), 0, 2) < 1).astype(jnp.int32), jax.random.fold_in(key_list[5], 1), 0, 1),
    }


threshold = 0.2
degree_floor = 0.25

def directions(values, metric):
    scaled = values.astype(jnp.float32)[:, None, :] * metric[None, :, :]
    unit_norm = jnp.sqrt(lax.optimization_barrier(jnp.sum(scaled * scaled, axis=-1, keepdims=True)) + 1e-06)
    return (scaled / unit_norm, unit_norm)

def project_back(dir_grad, unit_dirs, unit_norm):
    return (dir_grad - unit_dirs * lax.optimization_barrier(jnp.sum(unit_dirs * dir_grad, axis=-1, keepdims=True))) / unit_norm

def scores_of(node_block, metric, anchor_dirs):
    unit_dirs, unit_norm = directions(node_block, metric)
    node_dirs = unit_dirs.reshape(node_block.shape[0], -1).astype(jnp.bfloat16)
    score = lax.dot_general(node_dirs, anchor_dirs, (((1,), (1,)), ((), ())), preferred_element_type=jnp.float32) / metric.shape[0]
    excess = jnp.maximum(score - threshold, jnp.float32(0.0))
    link_weights = excess * excess
    return (unit_dirs, unit_norm, node_dirs, excess, link_weights)

def reference(features, anchors, metric, classifier, labels, train_mask):
    head_count, feat_width = metric.shape
    anchor_count = anchors.shape[0]
    classes = classifier.shape[1]
    anchor_unit, anchor_norm = directions(anchors, metric)
    anchor_dirs = anchor_unit.reshape(anchor_count, -1).astype(jnp.bfloat16)
    blocks = features.reshape(N_DP, ROWS_DEV, feat_width)
    label_blocks = labels.reshape(N_DP, ROWS_DEV)
    mask_blocks = train_mask.reshape(N_DP, ROWS_DEV)

    def first_pass(node_block):
        link_weights = scores_of(node_block, metric, anchor_dirs)[4]
        totals = lax.dot_general(link_weights.astype(jnp.bfloat16), node_block, (((0,), (0,)), ((), ())), preferred_element_type=jnp.float32)
        return (totals, lax.optimization_barrier(jnp.sum(link_weights, axis=0)))
    totals, degrees = lax.map(first_pass, blocks)
    anchor_total = lax.optimization_barrier(jnp.sum(totals, axis=0))
    anchor_raw = lax.optimization_barrier(jnp.sum(degrees, axis=0))
    anchor_degree = anchor_raw + degree_floor
    anchor_means = (anchor_total / anchor_degree[:, None]).astype(jnp.bfloat16)

    def second_pass(inputs):
        node_block, own_labels, own_mask = inputs
        link_weights = scores_of(node_block, metric, anchor_dirs)[4]
        link_b = link_weights.astype(jnp.bfloat16)
        node_raw = lax.optimization_barrier(jnp.sum(link_weights, axis=1))
        node_degree = node_raw + degree_floor
        node_field = jnp.dot(link_b, anchor_means, preferred_element_type=jnp.float32) / node_degree[:, None]
        logits = jnp.dot(node_field, classifier, precision=lax.Precision.HIGHEST, preferred_element_type=jnp.float32)
        target = (own_labels[:, None] == jnp.arange(classes, dtype=jnp.int32)[None, :]).astype(jnp.float32)
        residual = own_mask.astype(jnp.float32)[:, None] * (logits - target)
        field_grad = jnp.dot(residual, classifier.T, precision=lax.Precision.HIGHEST, preferred_element_type=jnp.float32)
        node_grads = (field_grad / node_degree[:, None]).astype(jnp.bfloat16)
        degree_grads = (-lax.optimization_barrier(jnp.sum(field_grad * node_field, axis=1)) / node_degree).astype(jnp.bfloat16)
        mean_part = lax.dot_general(link_b, node_grads, (((0,), (0,)), ((), ())), preferred_element_type=jnp.float32)
        class_part = lax.dot_general(node_field, residual, (((0,), (0,)), ((), ())), precision=lax.Precision.HIGHEST, preferred_element_type=jnp.float32)
        return (node_field.astype(jnp.bfloat16), node_grads, degree_grads, mean_part, class_part, 0.5 * jnp.sum(residual * residual))
    embedded, node_grads, degree_grads, mean_parts, class_parts, loss_parts = lax.map(second_pass, (blocks, label_blocks, mask_blocks))
    mean_grads = lax.optimization_barrier(jnp.sum(mean_parts, axis=0))
    grad_classifier = lax.optimization_barrier(jnp.sum(class_parts, axis=0))
    loss = jnp.sum(loss_parts) / (2.0 * NODES)
    total_grads = (mean_grads / anchor_degree[:, None]).astype(jnp.bfloat16)
    anchor_degree_grads = -lax.optimization_barrier(jnp.sum(mean_grads * anchor_total, axis=1)) / (anchor_degree * anchor_degree)

    def third_pass(inputs):
        node_block, block_grads, block_degree_grads = inputs
        unit_dirs, unit_norm, node_dirs, excess, link_weights = scores_of(node_block, metric, anchor_dirs)
        link_grads = lax.dot_general(block_grads, anchor_means, (((1,), (1,)), ((), ())), preferred_element_type=jnp.float32)
        link_grads = link_grads + lax.dot_general(node_block, total_grads, (((1,), (1,)), ((), ())), preferred_element_type=jnp.float32)
        link_grads = link_grads + block_degree_grads.astype(jnp.float32)[:, None] + anchor_degree_grads[None, :]
        score_grads = (link_grads * (2.0 / head_count) * excess).astype(jnp.bfloat16)
        anchor_part = lax.dot_general(score_grads, node_dirs, (((0,), (0,)), ((), ())), preferred_element_type=jnp.float32)
        node_dir_grads = jnp.dot(score_grads, anchor_dirs, preferred_element_type=jnp.float32).reshape(node_block.shape[0], head_count, feat_width)
        node_g = project_back(node_dir_grads, unit_dirs, unit_norm)
        return (anchor_part, lax.optimization_barrier(jnp.sum(node_g * node_block.astype(jnp.float32)[:, None, :], axis=0)))
    anchor_parts, metric_parts = lax.map(third_pass, (blocks, node_grads, degree_grads))
    anchor_dir_grads = lax.optimization_barrier(jnp.sum(anchor_parts, axis=0)).reshape(anchor_count, head_count, feat_width)
    anchor_g = project_back(anchor_dir_grads, anchor_unit, anchor_norm)
    grad_anchors = lax.optimization_barrier(jnp.sum(anchor_g * metric[None, :, :], axis=1))
    grad_metric = lax.optimization_barrier(jnp.sum(anchor_g * anchors[:, None, :], axis=0)) + lax.optimization_barrier(jnp.sum(metric_parts, axis=0))
    embedding = embedded.reshape(NODES, feat_width)
    return (embedding, loss, grad_classifier, grad_anchors, grad_metric)
```

```python
import jax
import jax.numpy as jnp
from jax import lax
from jax.experimental import pallas as pl
from jax.experimental.pallas import tpu as pltpu
from jax.sharding import Mesh
from jax.sharding import PartitionSpec as P

f32, bf16 = jnp.float32, jnp.bfloat16

threshold = 0.2
degree_floor = 0.25
F = 128
HEADS = 4
CLASSES = 172
CPAD = 256
OWN = 512
APD = 128
NZ = 8
VMEM = 48 * 1024 * 1024

NN = ((1,), (0,))
NT = ((1,), (1,))
TN = ((0,), (0,))


def mm(a, b, dims, precision=None):
    return lax.dot_general(a, b, (dims, ((), ())), precision=precision, preferred_element_type=f32)


def params(**kw):
    return pltpu.CompilerParams(vmem_limit_bytes=VMEM, **kw)


def vspec():
    return pl.BlockSpec(memory_space=pltpu.VMEM)


def column(row):
    return jnp.broadcast_to(row, (row.shape[1], row.shape[1])).T


def anchor_rows(anchors, metric, h):
    m = metric[h : h + 1, :]
    u = anchors * m
    r = lax.rsqrt(jnp.sum(u * u, axis=1, keepdims=True) + 1e-06)
    return u, r, m


def scaled_dirs(anchors, metric):
    rows = []
    for h in range(HEADS):
        u, r, m = anchor_rows(anchors, metric, h)
        rows.append((u * r * (m * (1.0 / HEADS))).astype(bf16))
    return jnp.concatenate(rows, axis=0)


def head_scores(am, ft, rinv):
    prod = mm(am, ft, NN)
    return [prod[h * APD : (h + 1) * APD, :] * rinv[h : h + 1, :] for h in range(HEADS)]


def excess_of(parts):
    score = (parts[0] + parts[1]) + (parts[2] + parts[3])
    return jnp.maximum(score - threshold, 0.0)


LINK_BLOCK = 1024
CHUNK = 256


def link_kernel(f_ref, a_ref, m_ref, ft_ref, rinv_ref, lb_ref, am_ref, msg_ref, tot, raw, m2c):
    i = pl.program_id(0)

    @pl.when(i == 0)
    def _():
        am_ref[...] = scaled_dirs(a_ref[...], m_ref[...])
        for h in range(HEADS):
            m = m_ref[h : h + 1, :]
            m2c[h] = column(m * m)
        tot[...] = jnp.zeros_like(tot)
        raw[...] = jnp.zeros_like(raw)

    for j in range(LINK_BLOCK // CHUNK):
        cols = slice(j * CHUNK, (j + 1) * CHUNK)
        ft = f_ref[cols, :].astype(f32).T
        ft_b = ft.astype(bf16)
        ft_ref[:, cols] = ft_b
        sq = ft * ft
        norms = []
        for h in range(HEADS):
            m2 = jnp.concatenate([m2c[h]] * (CHUNK // F), axis=1)
            norms.append(jnp.sum(sq * m2, axis=0, keepdims=True))
        rinv = lax.rsqrt(jnp.concatenate(norms + norms, axis=0) + 1e-06)
        rinv_ref[:, cols] = rinv
        e = excess_of(head_scores(am_ref[...], ft_b, rinv))
        link = e * e
        lb_ref[:, cols] = link.astype(bf16)
        raw[...] += sum(link[:, k * F : (k + 1) * F] for k in range(CHUNK // F))
    tot[...] += mm(lb_ref[...], f_ref[...], NN)

    @pl.when(i == pl.num_programs(0) - 1)
    def _():
        msg_ref[0:APD, :] = tot[...].astype(bf16)
        t = raw[...].T
        msg_ref[APD : APD + 16, :] = sum(t[16 * k : 16 * k + 16, :] for k in range(8)).astype(bf16)


def link_call(features, anchors, metric):
    n = features.shape[0]
    const = lambda i: (0, 0)
    return pl.pallas_call(
        link_kernel,
        grid=(n // LINK_BLOCK,),
        in_specs=[
            pl.BlockSpec((LINK_BLOCK, F), lambda i: (i, 0)),
            pl.BlockSpec((APD, F), const),
            pl.BlockSpec((HEADS, F), const),
        ],
        out_specs=[
            pl.BlockSpec((F, LINK_BLOCK), lambda i: (0, i)),
            pl.BlockSpec((8, LINK_BLOCK), lambda i: (0, i)),
            pl.BlockSpec((APD, LINK_BLOCK), lambda i: (0, i)),
            pl.BlockSpec((HEADS * APD, F), const),
            pl.BlockSpec((APD + 16, F), const),
        ],
        out_shape=[
            jax.ShapeDtypeStruct((F, n), bf16),
            jax.ShapeDtypeStruct((8, n), f32),
            jax.ShapeDtypeStruct((APD, n), bf16),
            jax.ShapeDtypeStruct((HEADS * APD, F), bf16),
            jax.ShapeDtypeStruct((APD + 16, F), bf16),
        ],
        scratch_shapes=[
            pltpu.VMEM((APD, F), f32),
            pltpu.VMEM((APD, F), f32),
            pltpu.VMEM((HEADS, F, F), f32),
        ],
        compiler_params=params(),
    )(features, anchors, metric)


def four(a, b, c, d):
    return (a[...].astype(f32) + b[...].astype(f32)) + (c[...].astype(f32) + d[...].astype(f32))


def mean_kernel(a, b, c, d, total_ref, degree_ref, means_ref):
    s = four(a, b, c, d)
    total = s[0:APD, :]
    degree = column(jnp.sum(s[APD:, :], axis=0, keepdims=True) + degree_floor)
    total_ref[...] = total
    degree_ref[...] = degree
    means = (total / degree).astype(bf16)
    for z in range(NZ):
        means_ref[z] = means


def mean_call(parts):
    return pl.pallas_call(
        mean_kernel,
        in_specs=[vspec()] * 4,
        out_specs=[vspec()] * 3,
        out_shape=[
            jax.ShapeDtypeStruct((APD, F), f32),
            jax.ShapeDtypeStruct((APD, F), f32),
            jax.ShapeDtypeStruct((NZ, APD, F), bf16),
        ],
        compiler_params=params(),
    )(*parts)


def head_kernel(s_ref, all_ref, m_ref, ft_ref, rinv_ref, ma_ref, mb_ref, cls_ref, lab_ref, mask_ref, emb_ref, msg_ref):
    core = lax.rem(s_ref[0], 2)
    metric = m_ref[...]
    ft = ft_ref[...]
    rinv = rinv_ref[...]

    def links(z, which, means_ref, field, raw):
        shard = 2 * z + which
        rows = pl.ds(pl.multiple_of(shard * APD, APD), APD)
        am = scaled_dirs(all_ref[rows, :], metric)
        e = excess_of(head_scores(am, ft, rinv))
        link = e * e
        field = field + mm(means_ref[z], link.astype(bf16), TN)
        raw = raw + sum(link[8 * k : 8 * k + 8, :] for k in range(APD // 8))
        return field, raw

    def step(z, carry):
        field, raw = links(z, core, ma_ref, *carry)
        return links(z, 1 - core, mb_ref, field, raw)

    field, raw = lax.fori_loop(0, NZ, step, (jnp.zeros((F, OWN), f32), jnp.zeros((8, OWN), f32)))
    inv_degree = 1.0 / (jnp.sum(raw, axis=0, keepdims=True) + degree_floor)
    field = field * inv_degree
    emb_ref[...] = field.T.astype(bf16)
    highest = lax.Precision.HIGHEST
    cls_t = cls_ref[...]
    logits = mm(cls_t, field, NN, highest)
    ids = lax.broadcasted_iota(jnp.int32, (CPAD, OWN), 0)
    target = jnp.where(ids == lab_ref[...], 1.0, 0.0)
    residual = mask_ref[...].astype(f32) * (logits - target)
    loss_row = jnp.sum(residual * residual, axis=0, keepdims=True)
    loss_row = sum(loss_row[:, k * F : (k + 1) * F] for k in range(OWN // F))
    class_part = mm(residual, field, NT, highest).astype(bf16)
    field_grad = mm(cls_t.T, residual, NN, highest)
    node_grads = (field_grad * inv_degree).astype(bf16)
    degree_grads = -jnp.sum(field_grad * field, axis=0, keepdims=True) * inv_degree
    small = jnp.concatenate(
        [degree_grads[:, k * F : (k + 1) * F] for k in range(OWN // F)] + [loss_row, jnp.zeros((11, F), f32)], axis=0
    ).astype(bf16)
    empty = jnp.zeros((16, F), bf16)
    for z in range(NZ):
        msg_ref[z, 0:F, :] = node_grads
        msg_ref[z, F : F + 16, 0:F] = class_part[32 * z : 32 * z + 16, :]
        msg_ref[z, F : F + 16, F : 2 * F] = class_part[32 * z + 16 : 32 * z + 32, :]
        msg_ref[z, F : F + 16, 2 * F : 3 * F] = small
        msg_ref[z, F : F + 16, 3 * F : 4 * F] = empty


def head_call(shard, anchors_all, metric, ft, rinv, means_a, means_b, cls_t, labels, mask):
    zero2 = lambda i, s: (0, 0)
    zero3 = lambda i, s: (0, 0, 0)
    own = lambda i, s: (0, s[0])
    return pl.pallas_call(
        head_kernel,
        grid_spec=pltpu.PrefetchScalarGridSpec(
            num_scalar_prefetch=1,
            grid=(1,),
            in_specs=[
                pl.BlockSpec(anchors_all.shape, zero2),
                pl.BlockSpec((HEADS, F), zero2),
                pl.BlockSpec((F, OWN), own),
                pl.BlockSpec((8, OWN), own),
                pl.BlockSpec((NZ, APD, F), zero3),
                pl.BlockSpec((NZ, APD, F), zero3),
                pl.BlockSpec((CPAD, F), zero2),
                pl.BlockSpec((1, OWN), own),
                pl.BlockSpec((1, OWN), own),
            ],
            out_specs=[
                pl.BlockSpec((OWN, F), zero2),
                pl.BlockSpec((NZ, F + 16, OWN), zero3),
            ],
        ),
        out_shape=[
            jax.ShapeDtypeStruct((OWN, F), bf16),
            jax.ShapeDtypeStruct((NZ, F + 16, OWN), bf16),
        ],
        compiler_params=params(),
    )(shard, anchors_all, metric, ft, rinv, means_a, means_b, cls_t, labels, mask)


def mean_grad_kernel(s_ref, lb_ref, ga_ref, gb_ref, msg_ref, loss_ref):
    core = lax.rem(s_ref[0], 2)
    grads = jnp.zeros((APD, F), f32)
    for z in range(NZ):
        for which, ref in ((core, ga_ref), (1 - core, gb_ref)):
            cols = pl.ds(pl.multiple_of((2 * z + which) * OWN, OWN), OWN)
            grads = grads + mm(lb_ref[:, cols], ref[z, 0:F, :], NT)
    msg_ref[0:APD, :] = grads.astype(bf16)
    extra = []
    for ref in (ga_ref, gb_ref):
        s = ref[0, F : F + 16, :].astype(f32)
        for z in range(1, NZ):
            s = s + ref[z, F : F + 16, :].astype(f32)
        extra.append(s)
    extra = extra[0] + extra[1]
    msg_ref[APD : APD + 16, :] = extra[:, 0:F].astype(bf16)
    msg_ref[APD + 16 : APD + 32, :] = extra[:, F : 2 * F].astype(bf16)
    loss_ref[...] = extra[0:8, 2 * F : 3 * F]


def mean_grad_call(shard, lb, grads_a, grads_b):
    return pl.pallas_call(
        mean_grad_kernel,
        in_specs=[pl.BlockSpec(memory_space=pltpu.SMEM)] + [vspec()] * 3,
        out_specs=[vspec()] * 2,
        out_shape=[
            jax.ShapeDtypeStruct((APD + 32, F), bf16),
            jax.ShapeDtypeStruct((8, F), f32),
        ],
        compiler_params=params(),
    )(shard, lb, grads_a, grads_b)


def score_kernel(
    s_ref, f0_ref, f1_ref, ft0_ref, ft1_ref, r0_ref, r1_ref, ga_ref, gb_ref, am_ref, a_ref, m_ref, means_ref, total_ref, degree_ref, loss_ref,
    p0, p1, p2, p3, msg_ref, cls_ref, acc, vacc, tg, adg, sgr
):
    i = pl.program_id(0)

    @pl.when(i == 0)
    def _():
        s = four(p0, p1, p2, p3)
        cls_ref[...] = s[APD:, :]
        grads = s[0:APD, :]
        inv = 1.0 / degree_ref[...]
        tg[...] = (grads * inv).astype(bf16)
        dots = jnp.sum(grads * total_ref[...], axis=1, keepdims=True)
        adg[...] = -dots * (inv * inv)
        acc[...] = jnp.zeros_like(acc)
        vacc[...] = jnp.zeros_like(vacc)

    am = am_ref[...]
    for f_ref, ft_ref, r_ref, g_ref in ((f0_ref, ft0_ref, r0_ref, ga_ref), (f1_ref, ft1_ref, r1_ref, gb_ref)):
        rows = []
        for j in range(OWN // CHUNK):
            cols = slice(j * CHUNK, (j + 1) * CHUNK)
            ft = ft_ref[:, cols]
            rinv = r_ref[:, cols]
            dg = jnp.concatenate([g_ref[0, F : F + 16, 2 * F : 3 * F].astype(f32)[k : k + 1, :] for k in range(2 * j, 2 * j + 2)], axis=1)
            parts = head_scores(am, ft, rinv)
            e = excess_of(parts)
            link_grads = mm(means_ref[...], g_ref[0, 0:F, cols], NN) + mm(tg[...], ft, NN)
            link_grads = link_grads + dg + jnp.concatenate([adg[...]] * (CHUNK // F), axis=1)
            sg = link_grads * (2.0 / HEADS) * e
            ws = []
            for h in range(HEADS):
                r = rinv[h : h + 1, :]
                sgr[h * APD : (h + 1) * APD, cols] = (sg * r).astype(bf16)
                ws.append(jnp.sum(sg * parts[h], axis=0, keepdims=True) * (r * r))
            w = jnp.concatenate(ws, axis=0)
            hi = w.astype(bf16).astype(f32)
            rows.append(jnp.concatenate([hi, w - hi], axis=0))
        v = jnp.concatenate(rows, axis=1).astype(bf16)
        fb = f_ref[...]
        acc[...] += mm(sgr[...], fb, NN)
        sq = fb.astype(f32)
        sq = sq * sq
        sq_hi = sq.astype(bf16)
        sq_lo = (sq - sq_hi.astype(f32)).astype(bf16)
        vacc[...] += mm(v, sq_hi, NN) + mm(v, sq_lo, NN)

    @pl.when(i == pl.num_programs(0) - 1)
    def _():
        anchors = a_ref[...]
        metric = m_ref[...]
        out = jnp.zeros((APD, F), f32)
        rows = []
        for h in range(HEADS):
            u, r, m = anchor_rows(anchors, metric, h)
            unit = u * r
            raw = acc[h * APD : (h + 1) * APD, :]
            grad = raw * m
            g = (grad - unit * jnp.sum(unit * grad, axis=1, keepdims=True)) * r
            out = out + g * m
            dirs = am_ref[h * APD : (h + 1) * APD, :].astype(f32)
            along = vacc[h : h + 1, :] + vacc[HEADS + h : HEADS + h + 1, :]
            row = jnp.sum(g * anchors, axis=0, keepdims=True)
            row = row + jnp.sum(dirs * raw, axis=0, keepdims=True) * (HEADS / m)
            rows.append(row - (m * HEADS) * along)
        msg_ref[0:APD, :] = out.astype(bf16)
        rows.append(loss_ref[4:5, :])
        rows.append(jnp.zeros((11, F), f32))
        msg_ref[APD : APD + 16, :] = jnp.concatenate(rows, axis=0).astype(bf16)


def score_call(shard, features, ft, rinv, grads_a, grads_b, am, anchors, metric, means, total, degree, loss, parts):
    n = features.shape[0]
    near = lambda i, s: 2 * i + s[0] % 2
    far = lambda i, s: 2 * i + 1 - s[0] % 2
    c2 = lambda i, s: (0, 0)
    whole = lambda x: pl.BlockSpec(x.shape, c2)
    return pl.pallas_call(
        score_kernel,
        grid_spec=pltpu.PrefetchScalarGridSpec(
            num_scalar_prefetch=1,
            grid=(NZ,),
            in_specs=[
                pl.BlockSpec((OWN, F), lambda i, s: (near(i, s), 0)),
                pl.BlockSpec((OWN, F), lambda i, s: (far(i, s), 0)),
                pl.BlockSpec((F, OWN), lambda i, s: (0, near(i, s))),
                pl.BlockSpec((F, OWN), lambda i, s: (0, far(i, s))),
                pl.BlockSpec((8, OWN), lambda i, s: (0, near(i, s))),
                pl.BlockSpec((8, OWN), lambda i, s: (0, far(i, s))),
                pl.BlockSpec((1, F + 16, OWN), lambda i, s: (i, 0, 0)),
                pl.BlockSpec((1, F + 16, OWN), lambda i, s: (i, 0, 0)),
                whole(am),
                whole(anchors),
                whole(metric),
                whole(means),
                whole(total),
                whole(degree),
                whole(loss),
            ]
            + [whole(p) for p in parts],
            out_specs=[pl.BlockSpec((APD + 16, F), c2), pl.BlockSpec((32, F), c2)],
            scratch_shapes=[
                pltpu.VMEM((HEADS * APD, F), f32),
                pltpu.VMEM((8, F), f32),
                pltpu.VMEM((APD, F), bf16),
                pltpu.VMEM((APD, F), f32),
                pltpu.VMEM((HEADS * APD, OWN), bf16),
            ],
        ),
        out_shape=[
            jax.ShapeDtypeStruct((APD + 16, F), bf16),
            jax.ShapeDtypeStruct((32, F), f32),
        ],
        compiler_params=params(),
    )(shard, features, features, ft, ft, rinv, rinv, grads_a, grads_b, am, anchors, metric, means, total, degree, loss, *parts)


def last_kernel(scale, p0, p1, p2, p3, cls_ref, out_ref, loss_ref, msg_ref):
    s = four(p0, p1, p2, p3)
    out_ref[...] = s[0:APD, :]
    loss_ref[...] = jnp.sum(s[APD + 4 : APD + 5, :], axis=1, keepdims=True) * scale
    for k in range(2 * NZ):
        msg_ref[k, 0:8, :] = s[APD : APD + 8, :]
        msg_ref[k, 8:40, :] = cls_ref[...]


def last_call(parts, cls, scale):
    return pl.pallas_call(
        lambda *refs: last_kernel(scale, *refs),
        in_specs=[vspec()] * 5,
        out_specs=[vspec()] * 3,
        out_shape=[
            jax.ShapeDtypeStruct((APD, F), f32),
            jax.ShapeDtypeStruct((1, 1), f32),
            jax.ShapeDtypeStruct((2 * NZ, 40, F), f32),
        ],
        compiler_params=params(),
    )(*parts, cls)


def finish_kernel(x_ref, metric_ref, cls_ref):
    s = x_ref[0, 0:8, :]
    for k in range(1, 2 * NZ):
        s = s + x_ref[k, 0:8, :]
    metric_ref[...] = s[0:HEADS, :]
    for z in range(NZ):
        rows = min(32, CLASSES - 32 * z)
        if rows > 0:
            cls_ref[32 * z : 32 * z + rows, :] = x_ref[2 * z, 8 : 8 + rows, :]


def finish_call(x):
    return pl.pallas_call(
        finish_kernel,
        in_specs=[vspec()],
        out_specs=[vspec()] * 2,
        out_shape=[jax.ShapeDtypeStruct((HEADS, F), f32), jax.ShapeDtypeStruct((CLASSES, F), f32)],
        compiler_params=params(),
    )(x)


def swap(x):
    return lax.ppermute(x, "c", [(0, 1), (1, 0)])


def shared(x, axis):
    others = [lax.ppermute(x, axis, [(i, i ^ k) for i in range(4)]) for k in (1, 2, 3)]
    return [x] + others


def sum4(parts):
    a, b, c, d = (p.astype(f32) for p in parts)
    return ((a + b) + (c + d)).astype(bf16)


def over_dp(x):
    return shared(sum4(shared(x, "x")), "y")


def body(features, anchors, metric, classifier, labels, train_mask):
    n = features.shape[0]
    shard = (lax.axis_index("z") * 2 + lax.axis_index("c")).astype(jnp.int32).reshape(1)
    anchors_all = lax.all_gather(anchors, ("z", "c"), tiled=True)
    cls_t = jnp.pad(classifier.T, ((0, CPAD - CLASSES), (0, 0)))
    ft, rinv, lb, am, msg = link_call(features, anchors, metric)
    total, degree, means8 = mean_call(over_dp(msg))
    means_a = lax.all_to_all(means8, "z", 0, 0, tiled=True)
    means_b = swap(means_a)
    embedding, msg = head_call(
        shard, anchors_all, metric, ft, rinv, means_a, means_b, cls_t, labels.reshape(1, n), train_mask.reshape(1, n)
    )
    grads_a = lax.all_to_all(msg, "z", 0, 0, tiled=True)
    grads_b = swap(grads_a)
    msg, loss = mean_grad_call(shard, lb, grads_a, grads_b)
    msg, cls = score_call(
        shard, features, ft, rinv, grads_a, grads_b, am, anchors, metric, means8[0], total, degree, loss, over_dp(msg)
    )
    grad_anchors, loss, msg = last_call(over_dp(msg), cls, 1.0 / (4.0 * n * 16))
    grad_metric, grad_cls = finish_call(lax.all_to_all(msg, ("z", "c"), 0, 0, tiled=True))
    return (embedding, loss.reshape(()), grad_cls.T, grad_anchors, grad_metric)


def solution(mesh):
    grid = Mesh(mesh.devices.reshape(4, 4, 8, 2), ("y", "x", "z", "c"))
    dp, sh = ("y", "x"), ("z", "c")
    return jax.shard_map(
        body,
        mesh=grid,
        in_specs=(P(dp, None), P(sh, None), P(), P(), P(dp), P(dp)),
        out_specs=(P(dp + sh, None), P(), P(), P(sh, None), P()),
        check_vma=False,
    )
```

```python
import jax
import jax.numpy as jnp
from jax import lax
from jax.experimental import pallas as pl
from jax.experimental.pallas import tpu as pltpu
from jax.sharding import Mesh
from jax.sharding import PartitionSpec as P

f32, bf16 = jnp.float32, jnp.bfloat16

threshold = 0.2
degree_floor = 0.25
F = 128
HEADS = 4
CLASSES = 172
CPAD = 256
OWN = 512
APD = 128
NZ = 8
MIB = 1024 * 1024

NN = ((1,), (0,))
NT = ((1,), (1,))
TN = ((0,), (0,))


def mm(a, b, dims, precision=None):
    return lax.dot_general(a, b, (dims, ((), ())), precision=precision, preferred_element_type=f32)


def params(mib=20):
    return pltpu.CompilerParams(vmem_limit_bytes=mib * MIB)


def vspec():
    return pl.BlockSpec(memory_space=pltpu.VMEM)


def column(row):
    return jnp.broadcast_to(row, (row.shape[1], row.shape[1])).T


def anchor_rows(anchors, metric, h):
    m = metric[h : h + 1, :]
    u = anchors * m
    r = lax.rsqrt(jnp.sum(u * u, axis=1, keepdims=True) + 1e-06)
    return u, r, m


def scaled_dirs(anchors, metric):
    rows = []
    for h in range(HEADS):
        u, r, m = anchor_rows(anchors, metric, h)
        rows.append((u * r * (m * (1.0 / HEADS))).astype(bf16))
    return jnp.concatenate(rows, axis=0)


def head_scores(am, ft, rinv):
    prod = mm(am, ft, NN)
    return [prod[h * APD : (h + 1) * APD, :] * rinv[h : h + 1, :] for h in range(HEADS)]


def excess_of(parts):
    score = (parts[0] + parts[1]) + (parts[2] + parts[3])
    return jnp.maximum(score - threshold, 0.0)


LINK_BLOCK = 1024
CHUNK = 256


def link_kernel(f_ref, a_ref, m_ref, ft_ref, rinv_ref, lb_ref, am_ref, msg_ref, tot, raw, m2c):
    i = pl.program_id(0)

    @pl.when(i == 0)
    def _():
        am_ref[...] = scaled_dirs(a_ref[...], m_ref[...])
        for h in range(HEADS):
            m = m_ref[h : h + 1, :]
            m2c[h] = column(m * m)
        tot[...] = jnp.zeros_like(tot)
        raw[...] = jnp.zeros_like(raw)

    for j in range(LINK_BLOCK // CHUNK):
        cols = slice(j * CHUNK, (j + 1) * CHUNK)
        ft = f_ref[cols, :].astype(f32).T
        ft_b = ft.astype(bf16)
        ft_ref[:, cols] = ft_b
        sq = ft * ft
        norms = []
        for h in range(HEADS):
            m2 = jnp.concatenate([m2c[h]] * (CHUNK // F), axis=1)
            norms.append(jnp.sum(sq * m2, axis=0, keepdims=True))
        rinv = lax.rsqrt(jnp.concatenate(norms + norms, axis=0) + 1e-06)
        rinv_ref[:, cols] = rinv
        e = excess_of(head_scores(am_ref[...], ft_b, rinv))
        link = e * e
        lb_ref[:, cols] = link.astype(bf16)
        raw[...] += sum(link[:, k * F : (k + 1) * F] for k in range(CHUNK // F))
    tot[...] += mm(lb_ref[...], f_ref[...], NN)

    @pl.when(i == pl.num_programs(0) - 1)
    def _():
        msg_ref[0:APD, :] = tot[...].astype(bf16)
        t = raw[...].T
        msg_ref[APD : APD + 16, :] = sum(t[16 * k : 16 * k + 16, :] for k in range(8)).astype(bf16)


def link_call(features, anchors, metric):
    n = features.shape[0]
    const = lambda i: (0, 0)
    return pl.pallas_call(
        link_kernel,
        grid=(n // LINK_BLOCK,),
        in_specs=[
            pl.BlockSpec((LINK_BLOCK, F), lambda i: (i, 0)),
            pl.BlockSpec((APD, F), const),
            pl.BlockSpec((HEADS, F), const),
        ],
        out_specs=[
            pl.BlockSpec((F, LINK_BLOCK), lambda i: (0, i)),
            pl.BlockSpec((8, LINK_BLOCK), lambda i: (0, i)),
            pl.BlockSpec((APD, LINK_BLOCK), lambda i: (0, i)),
            pl.BlockSpec((HEADS * APD, F), const),
            pl.BlockSpec((APD + 16, F), const),
        ],
        out_shape=[
            jax.ShapeDtypeStruct((F, n), bf16),
            jax.ShapeDtypeStruct((8, n), f32),
            jax.ShapeDtypeStruct((APD, n), bf16),
            jax.ShapeDtypeStruct((HEADS * APD, F), bf16),
            jax.ShapeDtypeStruct((APD + 16, F), bf16),
        ],
        scratch_shapes=[
            pltpu.VMEM((APD, F), f32),
            pltpu.VMEM((APD, F), f32),
            pltpu.VMEM((HEADS, F, F), f32),
        ],
        compiler_params=params(),
    )(features, anchors, metric)


def four(a, b, c, d):
    return (a[...].astype(f32) + b[...].astype(f32)) + (c[...].astype(f32) + d[...].astype(f32))


def mean_kernel(a, b, c, d, total_ref, degree_ref, means_ref):
    s = four(a, b, c, d)
    total = s[0:APD, :]
    degree = column(jnp.sum(s[APD:, :], axis=0, keepdims=True) + degree_floor)
    total_ref[...] = total
    degree_ref[...] = degree
    means = (total / degree).astype(bf16)
    for z in range(NZ):
        means_ref[z] = means


def mean_call(parts):
    return pl.pallas_call(
        mean_kernel,
        in_specs=[vspec()] * 4,
        out_specs=[vspec()] * 3,
        out_shape=[
            jax.ShapeDtypeStruct((APD, F), f32),
            jax.ShapeDtypeStruct((APD, F), f32),
            jax.ShapeDtypeStruct((NZ, APD, F), bf16),
        ],
        compiler_params=params(),
    )(*parts)


def head_kernel(s_ref, all_ref, m_ref, ft_ref, rinv_ref, ma_ref, mb_ref, cls_ref, lab_ref, mask_ref, emb_ref, up_ref, down_ref, part_ref, loss_ref):
    core = lax.rem(s_ref[0], 2)
    metric = m_ref[...]
    ft = ft_ref[...]
    rinv = rinv_ref[...]

    def links(z, which, means_ref, field, raw):
        shard = 2 * z + which
        rows = pl.ds(pl.multiple_of(shard * APD, APD), APD)
        am = scaled_dirs(all_ref[rows, :], metric)
        e = excess_of(head_scores(am, ft, rinv))
        link = e * e
        field = field + mm(means_ref[z], link.astype(bf16), TN)
        raw = raw + sum(link[8 * k : 8 * k + 8, :] for k in range(APD // 8))
        return field, raw

    def step(z, carry):
        field, raw = links(z, core, ma_ref, *carry)
        return links(z, 1 - core, mb_ref, field, raw)

    field, raw = lax.fori_loop(0, NZ, step, (jnp.zeros((F, OWN), f32), jnp.zeros((8, OWN), f32)))
    inv_degree = 1.0 / (jnp.sum(raw, axis=0, keepdims=True) + degree_floor)
    field = field * inv_degree
    emb_ref[...] = field.T.astype(bf16)
    highest = lax.Precision.HIGHEST
    cls_t = cls_ref[...]
    logits = mm(cls_t, field, NN, highest)
    ids = lax.broadcasted_iota(jnp.int32, (CPAD, OWN), 0)
    target = jnp.where(ids == lab_ref[...], 1.0, 0.0)
    residual = mask_ref[...].astype(f32) * (logits - target)
    loss_row = jnp.sum(residual * residual, axis=0, keepdims=True)
    loss_row = sum(loss_row[:, k * F : (k + 1) * F] for k in range(OWN // F))
    loss_ref[...] = jnp.concatenate([loss_row, jnp.zeros((7, F), f32)], axis=0)
    class_part = mm(residual, field, NT, highest)
    z = s_ref[0] // 2
    for k in range(NZ):
        part_ref[lax.rem(k - z + NZ, NZ)] = jnp.concatenate([class_part[32 * k + 8 * q : 32 * k + 8 * q + 8, :] for q in range(4)], axis=1)
    field_grad = mm(cls_t.T, residual, NN, highest)
    node_grads = (field_grad * inv_degree).astype(bf16)
    degree_grads = -jnp.sum(field_grad * field, axis=0, keepdims=True) * inv_degree
    for ref, k in ((up_ref, 4), (down_ref, 5)):
        ref[0:F, :] = node_grads
        ref[F : F + 16, :] = jnp.concatenate([degree_grads, jnp.zeros((7, OWN), f32), part_ref[k]], axis=0).astype(bf16)


def head_call(shard, anchors_all, metric, ft, rinv, means_a, means_b, cls_t, labels, mask):
    zero2 = lambda i, s: (0, 0)
    zero3 = lambda i, s: (0, 0, 0)
    own = lambda i, s: (0, s[0])
    return pl.pallas_call(
        head_kernel,
        grid_spec=pltpu.PrefetchScalarGridSpec(
            num_scalar_prefetch=1,
            grid=(1,),
            in_specs=[
                pl.BlockSpec(anchors_all.shape, zero2),
                pl.BlockSpec((HEADS, F), zero2),
                pl.BlockSpec((F, OWN), own),
                pl.BlockSpec((8, OWN), own),
                pl.BlockSpec((NZ, APD, F), zero3),
                pl.BlockSpec((NZ, APD, F), zero3),
                pl.BlockSpec((CPAD, F), zero2),
                pl.BlockSpec((1, OWN), own),
                pl.BlockSpec((1, OWN), own),
            ],
            out_specs=[
                pl.BlockSpec((OWN, F), zero2),
                pl.BlockSpec((F + 16, OWN), zero2),
                pl.BlockSpec((F + 16, OWN), zero2),
                pl.BlockSpec((NZ, 8, OWN), zero3),
                pl.BlockSpec((8, F), zero2),
            ],
        ),
        out_shape=[
            jax.ShapeDtypeStruct((OWN, F), bf16),
            jax.ShapeDtypeStruct((F + 16, OWN), bf16),
            jax.ShapeDtypeStruct((F + 16, OWN), bf16),
            jax.ShapeDtypeStruct((NZ, 8, OWN), f32),
            jax.ShapeDtypeStruct((8, F), f32),
        ],
        compiler_params=params(),
    )(shard, anchors_all, metric, ft, rinv, means_a, means_b, cls_t, labels, mask)


def mean_grad_kernel(s_ref, lb_ref, *refs):
    blocks, (msg_ref, all_ref) = refs[: 2 * NZ], refs[2 * NZ :]
    core = lax.rem(s_ref[0], 2)
    z = s_ref[0] // 2
    grads = jnp.zeros((APD, F), f32)
    for k, ref in enumerate(blocks):
        shard = 2 * lax.rem(z + k // 2, NZ) + (core if k % 2 == 0 else 1 - core)
        cols = pl.ds(pl.multiple_of(shard * OWN, OWN), OWN)
        all_ref[:, cols] = ref[...]
        grads = grads + mm(lb_ref[:, cols], ref[0:F, :], NT)
    msg_ref[...] = grads.astype(bf16)


def mean_grad_call(shard, lb, blocks):
    return pl.pallas_call(
        mean_grad_kernel,
        in_specs=[pl.BlockSpec(memory_space=pltpu.SMEM)] + [vspec()] * (1 + len(blocks)),
        out_specs=[vspec()] * 2,
        out_shape=[
            jax.ShapeDtypeStruct((APD, F), bf16),
            jax.ShapeDtypeStruct((F + 16, lb.shape[1]), bf16),
        ],
        compiler_params=params(),
    )(shard, lb, *blocks)


def score_kernel(
    f_ref, ft_ref, r_ref, g_ref, am_ref, a_ref, m_ref, means_ref, total_ref, degree_ref, loss_ref,
    p0, p1, p2, p3, msg_ref, acc, vacc, tg, adg, sgr
):
    i = pl.program_id(0)

    @pl.when(i == 0)
    def _():
        grads = four(p0, p1, p2, p3)
        inv = 1.0 / degree_ref[...]
        tg[...] = (grads * inv).astype(bf16)
        dots = jnp.sum(grads * total_ref[...], axis=1, keepdims=True)
        adg[...] = -dots * (inv * inv)
        acc[...] = jnp.zeros_like(acc)
        vacc[...] = jnp.zeros_like(vacc)

    am = am_ref[...]
    rows = []
    for j in range(SCORE_BLOCK // CHUNK):
        cols = slice(j * CHUNK, (j + 1) * CHUNK)
        ft = ft_ref[:, cols]
        rinv = r_ref[:, cols]
        dg = g_ref[F : F + 16, cols].astype(f32)[0:1, :]
        parts = head_scores(am, ft, rinv)
        e = excess_of(parts)
        link_grads = mm(means_ref[...], g_ref[0:F, cols], NN) + mm(tg[...], ft, NN)
        link_grads = link_grads + dg + jnp.concatenate([adg[...]] * (CHUNK // F), axis=1)
        sg = link_grads * (2.0 / HEADS) * e
        ws = []
        for h in range(HEADS):
            r = rinv[h : h + 1, :]
            sgr[h * APD : (h + 1) * APD, cols] = (sg * r).astype(bf16)
            ws.append(jnp.sum(sg * parts[h], axis=0, keepdims=True) * (r * r))
        w = jnp.concatenate(ws, axis=0)
        hi = w.astype(bf16).astype(f32)
        rows.append(jnp.concatenate([hi, w - hi], axis=0))
    v = jnp.concatenate(rows, axis=1).astype(bf16)
    fb = f_ref[...]
    acc[...] += mm(sgr[...], fb, NN)
    sq = fb.astype(f32)
    sq = sq * sq
    sq_hi = sq.astype(bf16)
    sq_lo = (sq - sq_hi.astype(f32)).astype(bf16)
    vacc[...] += mm(v, sq_hi, NN) + mm(v, sq_lo, NN)

    @pl.when(i == pl.num_programs(0) - 1)
    def _():
        anchors = a_ref[...]
        metric = m_ref[...]
        out = jnp.zeros((APD, F), f32)
        rows = []
        for h in range(HEADS):
            u, r, m = anchor_rows(anchors, metric, h)
            unit = u * r
            raw = acc[h * APD : (h + 1) * APD, :]
            grad = raw * m
            g = (grad - unit * jnp.sum(unit * grad, axis=1, keepdims=True)) * r
            out = out + g * m
            dirs = am_ref[h * APD : (h + 1) * APD, :].astype(f32)
            along = vacc[h : h + 1, :] + vacc[HEADS + h : HEADS + h + 1, :]
            row = jnp.sum(g * anchors, axis=0, keepdims=True)
            row = row + jnp.sum(dirs * raw, axis=0, keepdims=True) * (HEADS / m)
            rows.append(row - (m * HEADS) * along)
        msg_ref[0:APD, :] = out.astype(bf16)
        rows.append(loss_ref[0:1, :])
        rows.append(jnp.zeros((11, F), f32))
        msg_ref[APD : APD + 16, :] = jnp.concatenate(rows, axis=0).astype(bf16)


SCORE_BLOCK = 1024


def score_call(features, ft, rinv, grads, am, anchors, metric, means, total, degree, loss, parts):
    n = features.shape[0]
    c2 = lambda i: (0, 0)
    whole = lambda x: pl.BlockSpec(x.shape, c2)
    wide = lambda x: pl.BlockSpec((x.shape[0], SCORE_BLOCK), lambda i: (0, i))
    return pl.pallas_call(
        score_kernel,
        grid=(n // SCORE_BLOCK,),
        in_specs=[pl.BlockSpec((SCORE_BLOCK, F), lambda i: (i, 0)), wide(ft), wide(rinv), wide(grads)]
        + [whole(x) for x in (am, anchors, metric, means, total, degree, loss, *parts)],
        out_specs=pl.BlockSpec((APD + 16, F), c2),
        out_shape=jax.ShapeDtypeStruct((APD + 16, F), bf16),
        scratch_shapes=[
            pltpu.VMEM((HEADS * APD, F), f32),
            pltpu.VMEM((8, F), f32),
            pltpu.VMEM((APD, F), bf16),
            pltpu.VMEM((APD, F), f32),
            pltpu.VMEM((HEADS * APD, SCORE_BLOCK), bf16),
        ],
        compiler_params=params(),
    )(features, ft, rinv, grads, am, anchors, metric, means, total, degree, loss, *parts)


def last_kernel(p0, p1, p2, p3, out_ref, small_ref):
    s = four(p0, p1, p2, p3)
    out_ref[...] = s[0:APD, :]
    small_ref[0:8, :] = s[APD : APD + 8, :]
    small_ref[8:40, :] = s[APD + 16 : APD + 48, :]


def last_call(parts):
    return pl.pallas_call(
        last_kernel,
        in_specs=[vspec()] * 4,
        out_specs=[vspec()] * 2,
        out_shape=[
            jax.ShapeDtypeStruct((APD, F), f32),
            jax.ShapeDtypeStruct((40, F), f32),
        ],
        compiler_params=params(),
    )(*parts)


def finish_kernel(scale, x_ref, metric_ref, loss_ref, cls_ref):
    s = x_ref[0, 0:8, :]
    for k in range(1, NZ):
        s = s + x_ref[k, 0:8, :]
    metric_ref[...] = s[0:HEADS, :]
    loss_ref[...] = jnp.sum(s[HEADS : HEADS + 1, :], axis=1, keepdims=True) * scale
    for z in range(NZ):
        rows = min(32, CLASSES - 32 * z)
        if rows > 0:
            cls_ref[32 * z : 32 * z + rows, :] = x_ref[z, 8 : 8 + rows, :]


def finish_call(x, scale):
    return pl.pallas_call(
        lambda *refs: finish_kernel(scale, *refs),
        in_specs=[vspec()],
        out_specs=[vspec()] * 3,
        out_shape=[
            jax.ShapeDtypeStruct((HEADS, F), f32),
            jax.ShapeDtypeStruct((1, 1), f32),
            jax.ShapeDtypeStruct((CLASSES, F), f32),
        ],
        compiler_params=params(),
    )(x)


def swap(x):
    return lax.ppermute(x, "c", [(0, 1), (1, 0)])


def shared(x, axis):
    others = [lax.ppermute(x, axis, [(i, i ^ k) for i in range(4)]) for k in (1, 2, 3)]
    return [x] + others


def sum4(parts):
    a, b, c, d = (p.astype(f32) for p in parts)
    return ((a + b) + (c + d)).astype(bf16)


def over_dp(x):
    return shared(sum4(shared(x, "x")), "y")


def ring(up, down, part):
    ups, downs = [(i, (i + 1) % NZ) for i in range(NZ)], [(i, (i - 1) % NZ) for i in range(NZ)]

    def add(x, k):
        total = x[F + 8 :].astype(f32) + part[k]
        return jnp.concatenate([x[: F + 8], total.astype(bf16)], axis=0)

    blocks = [up] + [None] * (NZ - 1)
    for k in range(1, 5):
        up = lax.ppermute(up, "z", ups)
        blocks[NZ - k] = up
        if k < 4:
            down = lax.ppermute(down, "z", downs)
            blocks[k] = down
            up = add(up, 4 - k)
        if k < 3:
            down = add(down, 5 + k)
    total = (up[F + 8 :].astype(f32) + down[F + 8 :].astype(f32)) + part[0]
    return blocks, jnp.concatenate([total[:, q * F : (q + 1) * F] for q in range(4)], axis=0)


def body(features, anchors, metric, classifier, labels, train_mask):
    n = features.shape[0]
    shard = (lax.axis_index("z") * 2 + lax.axis_index("c")).astype(jnp.int32).reshape(1)
    anchors_all = lax.all_gather(anchors, ("z", "c"), tiled=True)
    cls_t = jnp.pad(classifier.T, ((0, CPAD - CLASSES), (0, 0)))
    ft, rinv, lb, am, msg = link_call(features, anchors, metric)
    total, degree, means8 = mean_call(over_dp(msg))
    means_a = lax.all_to_all(means8, "z", 0, 0, tiled=True)
    means_b = swap(means_a)
    embedding, up, down, part, loss = head_call(
        shard, anchors_all, metric, ft, rinv, means_a, means_b, cls_t, labels.reshape(1, n), train_mask.reshape(1, n)
    )
    blocks, cls = ring(up, down, part)
    blocks = [b for block in blocks for b in (block, swap(block))]
    msg, grads = mean_grad_call(shard, lb, blocks)
    msg = score_call(features, ft, rinv, grads, am, anchors, metric, means8[0], total, degree, loss, over_dp(msg))
    msg = jnp.concatenate([msg, cls.astype(bf16)], axis=0)
    grad_anchors, small = last_call(over_dp(msg))
    small = small + swap(small)
    small = lax.all_to_all(jnp.broadcast_to(small[None], (NZ,) + small.shape), "z", 0, 0, tiled=True)
    grad_metric, loss, grad_cls = finish_call(small, 1.0 / (4.0 * n * 16))
    return (embedding, loss.reshape(()), grad_cls.T, grad_anchors, grad_metric)


def solution(mesh):
    grid = Mesh(mesh.devices.reshape(4, 4, 8, 2), ("y", "x", "z", "c"))
    dp, sh = ("y", "x"), ("z", "c")
    return jax.shard_map(
        body,
        mesh=grid,
        in_specs=(P(dp, None), P(sh, None), P(), P(), P(dp), P(dp)),
        out_specs=(P(dp + sh, None), P(), P(), P(sh, None), P()),
        check_vma=False,
    )
```

```python
import jax
import jax.numpy as jnp
from jax import lax
from jax.experimental import pallas as pl
from jax.experimental.pallas import tpu as pltpu
from jax.sharding import Mesh
from jax.sharding import PartitionSpec as P

f32, bf16 = jnp.float32, jnp.bfloat16

threshold = 0.2
degree_floor = 0.25
F = 128
HEADS = 4
CLASSES = 172
CPAD = 256
OWN = 512
APD = 128
NZ = 8
MIB = 1024 * 1024

NN = ((1,), (0,))
NT = ((1,), (1,))
TN = ((0,), (0,))


def mm(a, b, dims, precision=None):
    return lax.dot_general(a, b, (dims, ((), ())), precision=precision, preferred_element_type=f32)


def params(mib=20):
    return pltpu.CompilerParams(vmem_limit_bytes=mib * MIB)


def vspec():
    return pl.BlockSpec(memory_space=pltpu.VMEM)


def column(row):
    return jnp.broadcast_to(row, (row.shape[1], row.shape[1])).T


def anchor_rows(anchors, metric, h):
    m = metric[h : h + 1, :]
    u = anchors * m
    r = lax.rsqrt(jnp.sum(u * u, axis=1, keepdims=True) + 1e-06)
    return u, r, m


def anchor_dirs(anchors, metric):
    rows = []
    for h in range(HEADS):
        u, r, _ = anchor_rows(anchors, metric, h)
        rows.append((u * (r * (1.0 / HEADS))).astype(bf16))
    return jnp.concatenate(rows, axis=1)


def node_dirs(ft, m_cols):
    dirs, norms = [], []
    for h in range(HEADS):
        u = ft * m_cols(h, ft.shape[1])
        r = lax.rsqrt(jnp.sum(u * u, axis=0, keepdims=True) + 1e-06)
        dirs.append((u * r).astype(bf16))
        norms.append(r)
    return jnp.concatenate(dirs, axis=0), jnp.concatenate(norms + norms, axis=0)


def wide_column(x, width):
    return jnp.concatenate([x] * (width // x.shape[1]), axis=1)


LINK_BLOCK = 1024
CHUNK = 256


def link_kernel(f_ref, a_ref, m_ref, lab_ref, mask_ref, ft_ref, rinv_ref, e_ref, lb_ref, tag_ref, am_ref, msg_ref, tot, raw, mc, ad):
    i = pl.program_id(0)

    @pl.when(i == 0)
    def _():
        anchors, metric = a_ref[...], m_ref[...]
        ad[...] = anchor_dirs(anchors, metric)
        for h in range(HEADS):
            u, r, m = anchor_rows(anchors, metric, h)
            am_ref[h * APD : (h + 1) * APD, :] = (u * r * m).astype(bf16)
            mc[h] = column(m)
        tot[...] = jnp.zeros_like(tot)
        raw[...] = jnp.zeros_like(raw)

    tag_ref[...] = jnp.where(mask_ref[...] > 0, lab_ref[...], -1)
    for j in range(LINK_BLOCK // CHUNK):
        cols = slice(j * CHUNK, (j + 1) * CHUNK)
        ft = f_ref[cols, :].astype(f32).T
        ft_ref[:, cols] = ft.astype(bf16)
        dirs, rinv = node_dirs(ft, lambda h, width: wide_column(mc[h], width))
        rinv_ref[:, cols] = rinv
        e = jnp.maximum(mm(ad[...], dirs, NN) - threshold, 0.0)
        link = e * e
        e_ref[:, cols] = e
        lb_ref[:, cols] = link.astype(bf16)
        raw[...] += sum(link[:, k * F : (k + 1) * F] for k in range(CHUNK // F))
    tot[...] += mm(lb_ref[...], f_ref[...], NN)

    @pl.when(i == pl.num_programs(0) - 1)
    def _():
        msg_ref[0:APD, :] = tot[...].astype(bf16)
        t = raw[...].T
        msg_ref[APD : APD + 16, :] = sum(t[16 * k : 16 * k + 16, :] for k in range(8)).astype(bf16)


def link_call(features, anchors, metric, labels, mask):
    n = features.shape[0]
    const = lambda i: (0, 0)
    wide = lambda rows: pl.BlockSpec((rows, LINK_BLOCK), lambda i: (0, i))
    return pl.pallas_call(
        link_kernel,
        grid=(n // LINK_BLOCK,),
        in_specs=[
            pl.BlockSpec((LINK_BLOCK, F), lambda i: (i, 0)),
            pl.BlockSpec((APD, F), const),
            pl.BlockSpec((HEADS, F), const),
            wide(1),
            wide(1),
        ],
        out_specs=[
            wide(F),
            wide(8),
            wide(APD),
            wide(APD),
            wide(1),
            pl.BlockSpec((HEADS * APD, F), const),
            pl.BlockSpec((APD + 16, F), const),
        ],
        out_shape=[
            jax.ShapeDtypeStruct((F, n), bf16),
            jax.ShapeDtypeStruct((8, n), f32),
            jax.ShapeDtypeStruct((APD, n), f32),
            jax.ShapeDtypeStruct((APD, n), bf16),
            jax.ShapeDtypeStruct((1, n), jnp.int32),
            jax.ShapeDtypeStruct((HEADS * APD, F), bf16),
            jax.ShapeDtypeStruct((APD + 16, F), bf16),
        ],
        scratch_shapes=[
            pltpu.VMEM((APD, F), f32),
            pltpu.VMEM((APD, F), f32),
            pltpu.VMEM((HEADS, F, F), f32),
            pltpu.VMEM((APD, HEADS * F), bf16),
        ],
        compiler_params=params(60),
    )(features, anchors, metric, labels, mask)


def four(a, b, c, d):
    return (a[...].astype(f32) + b[...].astype(f32)) + (c[...].astype(f32) + d[...].astype(f32))


def mean_kernel(a, b, c, d, anchors_ref, total_ref, degree_ref, means_ref, msg_ref):
    s = four(a, b, c, d)
    total = s[0:APD, :]
    degree = column(jnp.sum(s[APD:, :], axis=0, keepdims=True) + degree_floor)
    total_ref[...] = total
    degree_ref[...] = degree
    means = (total / degree).astype(bf16)
    means_ref[...] = means
    anchors = anchors_ref[...].astype(bf16)
    for z in range(NZ):
        msg_ref[z, 0:APD, :] = means
        msg_ref[z, APD:, :] = anchors


def mean_call(parts, anchors):
    return pl.pallas_call(
        mean_kernel,
        in_specs=[vspec()] * 5,
        out_specs=[vspec()] * 4,
        out_shape=[
            jax.ShapeDtypeStruct((APD, F), f32),
            jax.ShapeDtypeStruct((APD, F), f32),
            jax.ShapeDtypeStruct((APD, F), bf16),
            jax.ShapeDtypeStruct((NZ, 2 * APD, F), bf16),
        ],
        compiler_params=params(),
    )(*parts, anchors)


def head_kernel(s_ref, m_ref, ft_ref, ma_ref, mb_ref, cls_ref, tag_ref, emb_ref, up_ref, down_ref, part_ref, loss_ref):
    metric = m_ref[...]
    dirs, _ = node_dirs(ft_ref[...].astype(f32), lambda h, width: wide_column(column(metric[h : h + 1, :]), width))

    def step(z, carry):
        field, raw = carry
        for ref in (ma_ref, mb_ref):
            ad = anchor_dirs(ref[z, APD:, :].astype(f32), metric)
            e = jnp.maximum(mm(ad, dirs, NN) - threshold, 0.0)
            link = e * e
            field = field + mm(ref[z, 0:APD, :], link.astype(bf16), TN)
            raw = raw + sum(link[8 * k : 8 * k + 8, :] for k in range(APD // 8))
        return field, raw

    field, raw = lax.fori_loop(0, NZ, step, (jnp.zeros((F, OWN), f32), jnp.zeros((8, OWN), f32)))
    inv_degree = 1.0 / (jnp.sum(raw, axis=0, keepdims=True) + degree_floor)
    field = field * inv_degree
    emb_ref[...] = field.T.astype(bf16)
    highest = lax.Precision.HIGHEST
    cls_t = cls_ref[...]
    logits = mm(cls_t, field, NN, highest)
    ids = lax.broadcasted_iota(jnp.int32, (CPAD, OWN), 0)
    tag = tag_ref[...]
    residual = jnp.where(tag >= 0, logits - jnp.where(ids == tag, 1.0, 0.0), 0.0)
    loss_row = jnp.sum(residual * residual, axis=0, keepdims=True)
    loss_row = sum(loss_row[:, k * F : (k + 1) * F] for k in range(OWN // F))
    loss_ref[...] = jnp.concatenate([loss_row, jnp.zeros((7, F), f32)], axis=0)
    class_part = mm(residual, field, NT, highest)
    z = s_ref[0] // 2
    for k in range(NZ):
        part_ref[lax.rem(k - z + NZ, NZ)] = jnp.concatenate([class_part[32 * k + 8 * q : 32 * k + 8 * q + 8, :] for q in range(4)], axis=1)
    field_grad = mm(cls_t.T, residual, NN, highest)
    node_grads = (field_grad * inv_degree).astype(bf16)
    degree_grads = -jnp.sum(field_grad * field, axis=0, keepdims=True) * inv_degree
    for ref, k in ((up_ref, 4), (down_ref, 5)):
        ref[0:F, :] = node_grads
        ref[F : F + 16, :] = jnp.concatenate([degree_grads, jnp.zeros((7, OWN), f32), part_ref[k]], axis=0).astype(bf16)


def head_call(shard, metric, ft, means_a, means_b, cls_t, tags):
    zero2 = lambda i, s: (0, 0)
    zero3 = lambda i, s: (0, 0, 0)
    own = lambda i, s: (0, s[0])
    return pl.pallas_call(
        head_kernel,
        grid_spec=pltpu.PrefetchScalarGridSpec(
            num_scalar_prefetch=1,
            grid=(1,),
            in_specs=[
                pl.BlockSpec((HEADS, F), zero2),
                pl.BlockSpec((F, OWN), own),
                pl.BlockSpec((NZ, 2 * APD, F), zero3),
                pl.BlockSpec((NZ, 2 * APD, F), zero3),
                pl.BlockSpec((CPAD, F), zero2),
                pl.BlockSpec((1, OWN), own),
            ],
            out_specs=[
                pl.BlockSpec((OWN, F), zero2),
                pl.BlockSpec((F + 16, OWN), zero2),
                pl.BlockSpec((F + 16, OWN), zero2),
                pl.BlockSpec((NZ, 8, OWN), zero3),
                pl.BlockSpec((8, F), zero2),
            ],
        ),
        out_shape=[
            jax.ShapeDtypeStruct((OWN, F), bf16),
            jax.ShapeDtypeStruct((F + 16, OWN), bf16),
            jax.ShapeDtypeStruct((F + 16, OWN), bf16),
            jax.ShapeDtypeStruct((NZ, 8, OWN), f32),
            jax.ShapeDtypeStruct((8, F), f32),
        ],
        compiler_params=params(),
    )(shard, metric, ft, means_a, means_b, cls_t, tags)


def mean_grad_kernel(s_ref, lb_ref, *refs):
    blocks, (msg_ref, all_ref) = refs[: 2 * NZ], refs[2 * NZ :]
    core = lax.rem(s_ref[0], 2)
    z = s_ref[0] // 2
    grads = jnp.zeros((APD, F), f32)
    for k, ref in enumerate(blocks):
        shard = 2 * lax.rem(z + k // 2, NZ) + (core if k % 2 == 0 else 1 - core)
        cols = pl.ds(pl.multiple_of(shard * OWN, OWN), OWN)
        all_ref[:, cols] = ref[...]
        grads = grads + mm(lb_ref[:, cols], ref[0:F, :], NT)
    msg_ref[...] = grads.astype(bf16)


def mean_grad_call(shard, lb, blocks):
    return pl.pallas_call(
        mean_grad_kernel,
        in_specs=[pl.BlockSpec(memory_space=pltpu.SMEM)] + [vspec()] * (1 + len(blocks)),
        out_specs=[vspec()] * 2,
        out_shape=[
            jax.ShapeDtypeStruct((APD, F), bf16),
            jax.ShapeDtypeStruct((F + 16, lb.shape[1]), bf16),
        ],
        compiler_params=params(),
    )(shard, lb, *blocks)


def score_kernel(
    f_ref, ft_ref, r_ref, e_ref, g_ref, am_ref, a_ref, m_ref, means_ref, total_ref, degree_ref, loss_ref,
    p0, p1, p2, p3, msg_ref, acc, vacc, lhs, adg, sgr
):
    i = pl.program_id(0)

    @pl.when(i == 0)
    def _():
        grads = four(p0, p1, p2, p3)
        inv = 1.0 / degree_ref[...]
        lhs[:, 0:F] = means_ref[...] * 0.5
        lhs[:, F:] = (grads * inv).astype(bf16) * 0.5
        dots = jnp.sum(grads * total_ref[...], axis=1, keepdims=True)
        adg[...] = (-2.0 / HEADS) * dots * (inv * inv)
        acc[...] = jnp.zeros_like(acc)
        vacc[...] = jnp.zeros_like(vacc)

    rows = []
    for j in range(SCORE_BLOCK // CHUNK):
        cols = slice(j * CHUNK, (j + 1) * CHUNK)
        ft = ft_ref[:, cols]
        rinv = r_ref[:, cols]
        dg = g_ref[F : F + 16, cols].astype(f32)[0:1, :] * (2.0 / HEADS)
        link_grads = mm(lhs[...], jnp.concatenate([g_ref[0:F, cols], ft], axis=0), NN)
        sg = (link_grads + dg + wide_column(adg[...], CHUNK)) * e_ref[:, cols]
        ws = []
        for h in range(HEADS):
            r = rinv[h : h + 1, :]
            sgr[h * APD : (h + 1) * APD, cols] = (sg * r).astype(bf16)
            prod = mm(am_ref[h * APD : (h + 1) * APD, :], ft, NN)
            ws.append(jnp.sum(sg * prod, axis=0, keepdims=True) * (r * r * r))
        w = jnp.concatenate(ws, axis=0)
        hi = w.astype(bf16).astype(f32)
        rows.append(jnp.concatenate([hi, w - hi], axis=0))
    v = jnp.concatenate(rows, axis=1).astype(bf16)
    fb = f_ref[...]
    acc[...] += mm(sgr[...], fb, NN)
    sq = fb.astype(f32)
    sq = sq * sq
    sq_hi = sq.astype(bf16)
    sq_lo = (sq - sq_hi.astype(f32)).astype(bf16)
    vacc[...] += mm(v, sq_hi, NN) + mm(v, sq_lo, NN)

    @pl.when(i == pl.num_programs(0) - 1)
    def _():
        anchors = a_ref[...]
        metric = m_ref[...]
        out = jnp.zeros((APD, F), f32)
        rows = []
        for h in range(HEADS):
            u, r, m = anchor_rows(anchors, metric, h)
            unit = u * r
            raw = acc[h * APD : (h + 1) * APD, :]
            grad = raw * m
            g = (grad - unit * jnp.sum(unit * grad, axis=1, keepdims=True)) * r
            out = out + g * m
            dirs = am_ref[h * APD : (h + 1) * APD, :].astype(f32)
            along = vacc[h : h + 1, :] + vacc[HEADS + h : HEADS + h + 1, :]
            row = jnp.sum(g * anchors, axis=0, keepdims=True)
            row = row + jnp.sum(dirs * raw, axis=0, keepdims=True) / m
            rows.append(row - m * along)
        msg_ref[0:APD, :] = out.astype(bf16)
        rows.append(loss_ref[0:1, :])
        rows.append(jnp.zeros((11, F), f32))
        msg_ref[APD : APD + 16, :] = jnp.concatenate(rows, axis=0).astype(bf16)


SCORE_BLOCK = 1024


def score_call(features, ft, rinv, excess, grads, am, anchors, metric, means, total, degree, loss, parts):
    n = features.shape[0]
    c2 = lambda i: (0, 0)
    whole = lambda x: pl.BlockSpec(x.shape, c2)
    wide = lambda x: pl.BlockSpec((x.shape[0], SCORE_BLOCK), lambda i: (0, i))
    return pl.pallas_call(
        score_kernel,
        grid=(n // SCORE_BLOCK,),
        in_specs=[pl.BlockSpec((SCORE_BLOCK, F), lambda i: (i, 0)), wide(ft), wide(rinv), wide(excess), wide(grads)]
        + [whole(x) for x in (am, anchors, metric, means, total, degree, loss, *parts)],
        out_specs=pl.BlockSpec((APD + 16, F), c2),
        out_shape=jax.ShapeDtypeStruct((APD + 16, F), bf16),
        scratch_shapes=[
            pltpu.VMEM((HEADS * APD, F), f32),
            pltpu.VMEM((8, F), f32),
            pltpu.VMEM((APD, 2 * F), bf16),
            pltpu.VMEM((APD, F), f32),
            pltpu.VMEM((HEADS * APD, SCORE_BLOCK), bf16),
        ],
        compiler_params=params(),
    )(features, ft, rinv, excess, grads, am, anchors, metric, means, total, degree, loss, *parts)


def last_kernel(p0, p1, p2, p3, out_ref, small_ref):
    s = four(p0, p1, p2, p3)
    out_ref[...] = s[0:APD, :]
    small_ref[0:8, :] = s[APD : APD + 8, :]
    small_ref[8:40, :] = s[APD + 16 : APD + 48, :]


def last_call(parts):
    return pl.pallas_call(
        last_kernel,
        in_specs=[vspec()] * 4,
        out_specs=[vspec()] * 2,
        out_shape=[
            jax.ShapeDtypeStruct((APD, F), f32),
            jax.ShapeDtypeStruct((40, F), f32),
        ],
        compiler_params=params(),
    )(*parts)


def finish_kernel(scale, x_ref, metric_ref, loss_ref, cls_ref):
    s = x_ref[0, 0:8, :]
    for k in range(1, NZ):
        s = s + x_ref[k, 0:8, :]
    metric_ref[...] = s[0:HEADS, :]
    loss_ref[...] = jnp.sum(s[HEADS : HEADS + 1, :], axis=1, keepdims=True) * scale
    for z in range(NZ):
        rows = min(32, CLASSES - 32 * z)
        if rows > 0:
            cls_ref[32 * z : 32 * z + rows, :] = x_ref[z, 8 : 8 + rows, :]


def finish_call(x, scale):
    return pl.pallas_call(
        lambda *refs: finish_kernel(scale, *refs),
        in_specs=[vspec()],
        out_specs=[vspec()] * 3,
        out_shape=[
            jax.ShapeDtypeStruct((HEADS, F), f32),
            jax.ShapeDtypeStruct((1, 1), f32),
            jax.ShapeDtypeStruct((CLASSES, F), f32),
        ],
        compiler_params=params(),
    )(x)


def swap(x):
    return lax.ppermute(x, "c", [(0, 1), (1, 0)])


def shared(x, axis):
    others = [lax.ppermute(x, axis, [(i, i ^ k) for i in range(4)]) for k in (1, 2, 3)]
    return [x] + others


def sum4(parts):
    a, b, c, d = (p.astype(f32) for p in parts)
    return ((a + b) + (c + d)).astype(bf16)


def over_dp(x):
    return shared(sum4(shared(x, "x")), "y")


def ring(up, down, part):
    ups, downs = [(i, (i + 1) % NZ) for i in range(NZ)], [(i, (i - 1) % NZ) for i in range(NZ)]

    def add(x, k):
        total = x[F + 8 :].astype(f32) + part[k]
        return jnp.concatenate([x[: F + 8], total.astype(bf16)], axis=0)

    blocks = [up] + [None] * (NZ - 1)
    for k in range(1, 5):
        up = lax.ppermute(up, "z", ups)
        blocks[NZ - k] = up
        if k < 4:
            down = lax.ppermute(down, "z", downs)
            blocks[k] = down
            up = add(up, 4 - k)
        if k < 3:
            down = add(down, 5 + k)
    total = (up[F + 8 :].astype(f32) + down[F + 8 :].astype(f32)) + part[0]
    return blocks, jnp.concatenate([total[:, q * F : (q + 1) * F] for q in range(4)], axis=0)


def body(features, anchors, metric, classifier, labels, train_mask):
    n = features.shape[0]
    shard = (lax.axis_index("z") * 2 + lax.axis_index("c")).astype(jnp.int32).reshape(1)
    cls_t = jnp.pad(classifier.T, ((0, CPAD - CLASSES), (0, 0)))
    ft, rinv, excess, lb, tags, am, msg = link_call(features, anchors, metric, labels.reshape(1, n), train_mask.reshape(1, n))
    total, degree, means, msg = mean_call(over_dp(msg), anchors)
    means_a = lax.all_to_all(msg, "z", 0, 0, tiled=True)
    means_b = swap(means_a)
    embedding, up, down, part, loss = head_call(shard, metric, ft, means_a, means_b, cls_t, tags)
    blocks, cls = ring(up, down, part)
    blocks = [b for block in blocks for b in (block, swap(block))]
    msg, grads = mean_grad_call(shard, lb, blocks)
    msg = score_call(features, ft, rinv, excess, grads, am, anchors, metric, means, total, degree, loss, over_dp(msg))
    msg = jnp.concatenate([msg, cls.astype(bf16)], axis=0)
    grad_anchors, small = last_call(over_dp(msg))
    small = small + swap(small)
    small = lax.all_to_all(jnp.broadcast_to(small[None], (NZ,) + small.shape), "z", 0, 0, tiled=True)
    grad_metric, loss, grad_cls = finish_call(small, 1.0 / (4.0 * n * 16))
    return (embedding, loss.reshape(()), grad_cls.T, grad_anchors, grad_metric)


def solution(mesh):
    grid = Mesh(mesh.devices.reshape(4, 4, 8, 2), ("y", "x", "z", "c"))
    dp, sh = ("y", "x"), ("z", "c")
    return jax.shard_map(
        body,
        mesh=grid,
        in_specs=(P(dp, None), P(sh, None), P(), P(), P(dp), P(dp)),
        out_specs=(P(dp + sh, None), P(), P(), P(sh, None), P()),
        check_vma=False,
    )
```

```python
import jax
import jax.numpy as jnp
from jax import lax
from jax.experimental import pallas as pl
from jax.experimental.pallas import tpu as pltpu
from jax.sharding import Mesh
from jax.sharding import PartitionSpec as P

f32, bf16 = jnp.float32, jnp.bfloat16

threshold = 0.2
degree_floor = 0.25
F = 128
HEADS = 4
CLASSES = 172
CPAD = 256
OWN = 512
APD = 128
NZ = 8
MIB = 1024 * 1024

NN = ((1,), (0,))
NT = ((1,), (1,))
TN = ((0,), (0,))


def mm(a, b, dims, precision=None):
    return lax.dot_general(a, b, (dims, ((), ())), precision=precision, preferred_element_type=f32)


def params(mib=20):
    return pltpu.CompilerParams(vmem_limit_bytes=mib * MIB)


def vspec():
    return pl.BlockSpec(memory_space=pltpu.VMEM)


def column(row):
    return jnp.broadcast_to(row, (row.shape[1], row.shape[1])).T


def anchor_rows(anchors, metric, h):
    m = metric[h : h + 1, :]
    u = anchors * m
    r = lax.rsqrt(jnp.sum(u * u, axis=1, keepdims=True) + 1e-06)
    return u, r, m


def anchor_dirs(anchors, metric):
    rows = []
    for h in range(HEADS):
        u, r, _ = anchor_rows(anchors, metric, h)
        rows.append((u * (r * (1.0 / HEADS))).astype(bf16))
    return jnp.concatenate(rows, axis=1)


def node_dirs(ft, m_cols):
    dirs, norms = [], []
    for h in range(HEADS):
        u = ft * m_cols(h, ft.shape[1])
        r = lax.rsqrt(jnp.sum(u * u, axis=0, keepdims=True) + 1e-06)
        dirs.append((u * r).astype(bf16))
        norms.append(r)
    return jnp.concatenate(dirs, axis=0), jnp.concatenate(norms + norms, axis=0)


def wide_column(x, width):
    return jnp.concatenate([x] * (width // x.shape[1]), axis=1)


LINK_BLOCK = 2048
CHUNK = 256


def link_kernel(f_ref, a_ref, m_ref, lab_ref, mask_ref, ft_ref, rinv_ref, e_ref, lb_ref, tag_ref, am_ref, msg_ref, tot, raw, mc, ad):
    i = pl.program_id(0)

    @pl.when(i == 0)
    def _():
        anchors, metric = a_ref[...], m_ref[...]
        ad[...] = anchor_dirs(anchors, metric)
        for h in range(HEADS):
            u, r, m = anchor_rows(anchors, metric, h)
            am_ref[h * APD : (h + 1) * APD, :] = (u * r * m).astype(bf16)
            mc[h] = column(m)
        tot[...] = jnp.zeros_like(tot)
        raw[...] = jnp.zeros_like(raw)

    for j in range(LINK_BLOCK // CHUNK):
        cols = slice(j * CHUNK, (j + 1) * CHUNK)
        ft = f_ref[cols, :].astype(f32).T
        ft_ref[:, cols] = ft.astype(bf16)
        dirs, rinv = node_dirs(ft, lambda h, width: wide_column(mc[h], width))
        rinv_ref[:, cols] = rinv
        e = jnp.maximum(mm(ad[...], dirs, NN) - threshold, 0.0)
        link = e * e
        e_ref[:, cols] = e.astype(bf16)
        lb_ref[:, cols] = link.astype(bf16)
        raw[...] += sum(link[:, k * F : (k + 1) * F] for k in range(CHUNK // F))
    tot[...] += mm(lb_ref[...], f_ref[...], NN)
    tag_ref[...] = jnp.where(mask_ref[...] > 0, lab_ref[...], -1)

    @pl.when(i == pl.num_programs(0) - 1)
    def _():
        msg_ref[0:APD, :] = tot[...].astype(bf16)
        t = raw[...].T
        msg_ref[APD : APD + 16, :] = sum(t[16 * k : 16 * k + 16, :] for k in range(8)).astype(bf16)


def link_call(features, anchors, metric, labels, mask):
    n = features.shape[0]
    const = lambda i: (0, 0)
    wide = lambda rows: pl.BlockSpec((rows, LINK_BLOCK), lambda i: (0, i))
    return pl.pallas_call(
        link_kernel,
        grid=(n // LINK_BLOCK,),
        in_specs=[
            pl.BlockSpec((LINK_BLOCK, F), lambda i: (i, 0)),
            pl.BlockSpec((APD, F), const),
            pl.BlockSpec((HEADS, F), const),
            wide(1),
            wide(1),
        ],
        out_specs=[
            wide(F),
            wide(8),
            wide(APD),
            wide(APD),
            wide(1),
            pl.BlockSpec((HEADS * APD, F), const),
            pl.BlockSpec((APD + 16, F), const),
        ],
        out_shape=[
            jax.ShapeDtypeStruct((F, n), bf16),
            jax.ShapeDtypeStruct((8, n), f32),
            jax.ShapeDtypeStruct((APD, n), bf16),
            jax.ShapeDtypeStruct((APD, n), bf16),
            jax.ShapeDtypeStruct((1, n), jnp.int32),
            jax.ShapeDtypeStruct((HEADS * APD, F), bf16),
            jax.ShapeDtypeStruct((APD + 16, F), bf16),
        ],
        scratch_shapes=[
            pltpu.VMEM((APD, F), f32),
            pltpu.VMEM((APD, F), f32),
            pltpu.VMEM((HEADS, F, F), f32),
            pltpu.VMEM((APD, HEADS * F), bf16),
        ],
        compiler_params=params(60),
    )(features, anchors, metric, labels, mask)


def four(a, b, c, d):
    return (a[...].astype(f32) + b[...].astype(f32)) + (c[...].astype(f32) + d[...].astype(f32))


def mean_kernel(a, b, c, d, anchors_ref, total_ref, degree_ref, means_ref, msg_ref):
    s = four(a, b, c, d)
    total = s[0:APD, :]
    degree = column(jnp.sum(s[APD:, :], axis=0, keepdims=True) + degree_floor)
    total_ref[...] = total
    degree_ref[...] = degree
    means = (total / degree).astype(bf16)
    means_ref[...] = means
    anchors = anchors_ref[...].astype(bf16)
    for z in range(NZ):
        msg_ref[z, 0:APD, :] = means
        msg_ref[z, APD:, :] = anchors


def mean_call(parts, anchors):
    return pl.pallas_call(
        mean_kernel,
        in_specs=[vspec()] * 5,
        out_specs=[vspec()] * 4,
        out_shape=[
            jax.ShapeDtypeStruct((APD, F), f32),
            jax.ShapeDtypeStruct((APD, F), f32),
            jax.ShapeDtypeStruct((APD, F), bf16),
            jax.ShapeDtypeStruct((NZ, 2 * APD, F), bf16),
        ],
        compiler_params=params(),
    )(*parts, anchors)


HEAD_STEP = 2


def head_kernel(s_ref, m_ref, ft_ref, ma_ref, mb_ref, cls_ref, tag_ref, emb_ref, up_ref, down_ref, part_ref, loss_ref):
    metric = m_ref[...]
    dirs, _ = node_dirs(ft_ref[...].astype(f32), lambda h, width: wide_column(column(metric[h : h + 1, :]), width))

    def step(i, carry):
        field, raw = carry
        blocks = [ref[HEAD_STEP * i + k] for k in range(HEAD_STEP) for ref in (ma_ref, mb_ref)]
        ad = jnp.concatenate([anchor_dirs(b[APD:, :].astype(f32), metric) for b in blocks], axis=0)
        means = jnp.concatenate([b[0:APD, :] for b in blocks], axis=0)
        e = jnp.maximum(mm(ad, dirs, NN) - threshold, 0.0)
        link = e * e
        field = field + mm(means, link.astype(bf16), TN)
        raw = raw + sum(link[8 * k : 8 * k + 8, :] for k in range(link.shape[0] // 8))
        return field, raw

    field, raw = lax.fori_loop(0, NZ // HEAD_STEP, step, (jnp.zeros((F, OWN), f32), jnp.zeros((8, OWN), f32)))
    inv_degree = 1.0 / (jnp.sum(raw, axis=0, keepdims=True) + degree_floor)
    field = field * inv_degree
    emb_ref[...] = field.T.astype(bf16)
    highest = lax.Precision.HIGHEST
    cls_t = cls_ref[...]
    logits = mm(cls_t, field, NN, highest)
    ids = lax.broadcasted_iota(jnp.int32, (CPAD, OWN), 0)
    tag = tag_ref[...]
    residual = jnp.where(tag >= 0, logits - jnp.where(ids == tag, 1.0, 0.0), 0.0)
    loss_row = jnp.sum(residual * residual, axis=0, keepdims=True)
    loss_row = sum(loss_row[:, k * F : (k + 1) * F] for k in range(OWN // F))
    loss_ref[...] = jnp.concatenate([loss_row, jnp.zeros((7, F), f32)], axis=0)
    class_part = mm(residual, field, NT, highest)
    z = s_ref[0] // 2
    for k in range(NZ):
        part_ref[lax.rem(k - z + NZ, NZ)] = jnp.concatenate([class_part[32 * k + 8 * q : 32 * k + 8 * q + 8, :] for q in range(4)], axis=1)
    field_grad = mm(cls_t.T, residual, NN, highest)
    node_grads = (field_grad * inv_degree).astype(bf16)
    degree_grads = -jnp.sum(field_grad * field, axis=0, keepdims=True) * inv_degree
    for ref, k in ((up_ref, 4), (down_ref, 5)):
        ref[0:F, :] = node_grads
        ref[F : F + 16, :] = jnp.concatenate([degree_grads, jnp.zeros((7, OWN), f32), part_ref[k]], axis=0).astype(bf16)


def head_call(shard, *operands):
    return pl.pallas_call(
        head_kernel,
        in_specs=[pl.BlockSpec(memory_space=pltpu.SMEM)] + [vspec()] * len(operands),
        out_specs=[vspec()] * 5,
        out_shape=[
            jax.ShapeDtypeStruct((OWN, F), bf16),
            jax.ShapeDtypeStruct((F + 16, OWN), bf16),
            jax.ShapeDtypeStruct((F + 16, OWN), bf16),
            jax.ShapeDtypeStruct((NZ, 8, OWN), f32),
            jax.ShapeDtypeStruct((8, F), f32),
        ],
        compiler_params=params(),
    )(shard, *operands)


def mean_grad_kernel(s_ref, lb_ref, *refs):
    blocks, (msg_ref, all_ref) = refs[: 2 * NZ], refs[2 * NZ :]
    core = lax.rem(s_ref[0], 2)
    z = s_ref[0] // 2
    grads = jnp.zeros((APD, F), f32)
    for k, ref in enumerate(blocks):
        shard = 2 * lax.rem(z + k // 2, NZ) + (core if k % 2 == 0 else 1 - core)
        cols = pl.ds(pl.multiple_of(shard * OWN, OWN), OWN)
        all_ref[:, cols] = ref[...]
        grads = grads + mm(lb_ref[:, cols], ref[0:F, :], NT)
    msg_ref[...] = grads.astype(bf16)


def mean_grad_call(shard, lb, blocks):
    return pl.pallas_call(
        mean_grad_kernel,
        in_specs=[pl.BlockSpec(memory_space=pltpu.SMEM)] + [vspec()] * (1 + len(blocks)),
        out_specs=[vspec()] * 2,
        out_shape=[
            jax.ShapeDtypeStruct((APD, F), bf16),
            jax.ShapeDtypeStruct((F + 16, lb.shape[1]), bf16),
        ],
        compiler_params=params(),
    )(shard, lb, *blocks)


def score_kernel(
    f_ref, ft_ref, r_ref, e_ref, g_ref, am_ref, a_ref, m_ref, means_ref, total_ref, degree_ref, loss_ref,
    p0, p1, p2, p3, msg_ref, acc, vacc, lhs, adg, sgr
):
    i = pl.program_id(0)

    @pl.when(i == 0)
    def _():
        grads = four(p0, p1, p2, p3)
        inv = 1.0 / degree_ref[...]
        lhs[:, 0:F] = means_ref[...] * 0.5
        lhs[:, F:] = (grads * inv).astype(bf16) * 0.5
        dots = jnp.sum(grads * total_ref[...], axis=1, keepdims=True)
        adg[...] = (-2.0 / HEADS) * dots * (inv * inv)
        acc[...] = jnp.zeros_like(acc)
        vacc[...] = jnp.zeros_like(vacc)

    rows = []
    for j in range(SCORE_BLOCK // SCORE_CHUNK):
        cols = slice(j * SCORE_CHUNK, (j + 1) * SCORE_CHUNK)
        ft = ft_ref[:, cols]
        rinv = r_ref[:, cols]
        dg = g_ref[F : F + 16, cols].astype(f32)[0:1, :] * (2.0 / HEADS)
        link_grads = mm(lhs[...], jnp.concatenate([g_ref[0:F, cols], ft], axis=0), NN)
        sg = (link_grads + dg + wide_column(adg[...], SCORE_CHUNK)) * e_ref[:, cols].astype(f32)
        ws = []
        for h in range(HEADS):
            r = rinv[h : h + 1, :]
            sgr[h * APD : (h + 1) * APD, cols] = (sg * r).astype(bf16)
            prod = mm(am_ref[h * APD : (h + 1) * APD, :], ft, NN)
            ws.append(jnp.sum(sg * prod, axis=0, keepdims=True) * (r * r * r))
        w = jnp.concatenate(ws, axis=0)
        hi = w.astype(bf16).astype(f32)
        rows.append(jnp.concatenate([hi, w - hi], axis=0))
    v = jnp.concatenate(rows, axis=1).astype(bf16)
    fb = f_ref[...]
    acc[...] += mm(sgr[...], fb, NN)
    sq = fb.astype(f32)
    sq = sq * sq
    sq_hi = sq.astype(bf16)
    sq_lo = (sq - sq_hi.astype(f32)).astype(bf16)
    vacc[...] += mm(v, sq_hi, NN) + mm(v, sq_lo, NN)

    @pl.when(i == pl.num_programs(0) - 1)
    def _():
        anchors = a_ref[...]
        metric = m_ref[...]
        out = jnp.zeros((APD, F), f32)
        rows = []
        for h in range(HEADS):
            u, r, m = anchor_rows(anchors, metric, h)
            unit = u * r
            raw = acc[h * APD : (h + 1) * APD, :]
            grad = raw * m
            g = (grad - unit * jnp.sum(unit * grad, axis=1, keepdims=True)) * r
            out = out + g * m
            dirs = am_ref[h * APD : (h + 1) * APD, :].astype(f32)
            along = vacc[h : h + 1, :] + vacc[HEADS + h : HEADS + h + 1, :]
            row = jnp.sum(g * anchors, axis=0, keepdims=True)
            row = row + jnp.sum(dirs * raw, axis=0, keepdims=True) / m
            rows.append(row - m * along)
        msg_ref[0:APD, :] = out.astype(bf16)
        rows.append(loss_ref[0:1, :])
        rows.append(jnp.zeros((11, F), f32))
        msg_ref[APD : APD + 16, :] = jnp.concatenate(rows, axis=0).astype(bf16)


SCORE_BLOCK = 2048
SCORE_CHUNK = 256


def score_call(features, ft, rinv, excess, grads, am, anchors, metric, means, total, degree, loss, parts):
    n = features.shape[0]
    c2 = lambda i: (0, 0)
    whole = lambda x: pl.BlockSpec(x.shape, c2)
    wide = lambda x: pl.BlockSpec((x.shape[0], SCORE_BLOCK), lambda i: (0, i))
    return pl.pallas_call(
        score_kernel,
        grid=(n // SCORE_BLOCK,),
        in_specs=[pl.BlockSpec((SCORE_BLOCK, F), lambda i: (i, 0)), wide(ft), wide(rinv), wide(excess), wide(grads)]
        + [whole(x) for x in (am, anchors, metric, means, total, degree, loss, *parts)],
        out_specs=pl.BlockSpec((APD + 16, F), c2),
        out_shape=jax.ShapeDtypeStruct((APD + 16, F), bf16),
        scratch_shapes=[
            pltpu.VMEM((HEADS * APD, F), f32),
            pltpu.VMEM((8, F), f32),
            pltpu.VMEM((APD, 2 * F), bf16),
            pltpu.VMEM((APD, F), f32),
            pltpu.VMEM((HEADS * APD, SCORE_BLOCK), bf16),
        ],
        compiler_params=params(24),
    )(features, ft, rinv, excess, grads, am, anchors, metric, means, total, degree, loss, *parts)


def last_kernel(p0, p1, p2, p3, out_ref, small_ref):
    s = four(p0, p1, p2, p3)
    out_ref[...] = s[0:APD, :]
    small_ref[0:8, :] = s[APD : APD + 8, :]
    small_ref[8:40, :] = s[APD + 16 : APD + 48, :]


def last_call(parts):
    return pl.pallas_call(
        last_kernel,
        in_specs=[vspec()] * 4,
        out_specs=[vspec()] * 2,
        out_shape=[
            jax.ShapeDtypeStruct((APD, F), f32),
            jax.ShapeDtypeStruct((40, F), f32),
        ],
        compiler_params=params(),
    )(*parts)


def finish_kernel(scale, x_ref, metric_ref, loss_ref, cls_ref):
    s = x_ref[0, 0:8, :]
    for k in range(1, NZ):
        s = s + x_ref[k, 0:8, :]
    metric_ref[...] = s[0:HEADS, :]
    loss_ref[...] = jnp.sum(s[HEADS : HEADS + 1, :], axis=1, keepdims=True) * scale
    for z in range(NZ):
        rows = min(32, CLASSES - 32 * z)
        if rows > 0:
            cls_ref[32 * z : 32 * z + rows, :] = x_ref[z, 8 : 8 + rows, :]


def finish_call(x, scale):
    return pl.pallas_call(
        lambda *refs: finish_kernel(scale, *refs),
        in_specs=[vspec()],
        out_specs=[vspec()] * 3,
        out_shape=[
            jax.ShapeDtypeStruct((HEADS, F), f32),
            jax.ShapeDtypeStruct((1, 1), f32),
            jax.ShapeDtypeStruct((CLASSES, F), f32),
        ],
        compiler_params=params(),
    )(x)


def swap(x):
    return lax.ppermute(x, "c", [(0, 1), (1, 0)])


def shared(x, axis):
    others = [lax.ppermute(x, axis, [(i, i ^ k) for i in range(4)]) for k in (1, 2, 3)]
    return [x] + others


def sum4(parts):
    a, b, c, d = (p.astype(f32) for p in parts)
    return ((a + b) + (c + d)).astype(bf16)


def over_dp(x):
    return shared(sum4(shared(x, "x")), "y")


def ring(up, down, part):
    ups, downs = [(i, (i + 1) % NZ) for i in range(NZ)], [(i, (i - 1) % NZ) for i in range(NZ)]

    def add(x, k):
        total = x[F + 8 :].astype(f32) + part[k]
        return jnp.concatenate([x[: F + 8], total.astype(bf16)], axis=0)

    blocks = [up] + [None] * (NZ - 1)
    for k in range(1, 5):
        up = lax.ppermute(up, "z", ups)
        blocks[NZ - k] = up
        if k < 4:
            down = lax.ppermute(down, "z", downs)
            blocks[k] = down
            up = add(up, 4 - k)
        if k < 3:
            down = add(down, 5 + k)
    total = (up[F + 8 :].astype(f32) + down[F + 8 :].astype(f32)) + part[0]
    return blocks, jnp.concatenate([total[:, q * F : (q + 1) * F] for q in range(4)], axis=0)


def body(features, anchors, metric, classifier, labels, train_mask):
    n = features.shape[0]
    shard = (lax.axis_index("z") * 2 + lax.axis_index("c")).astype(jnp.int32).reshape(1)
    cls_t = jnp.pad(classifier.T, ((0, CPAD - CLASSES), (0, 0)))
    ft, rinv, excess, lb, tags, am, msg = link_call(features, anchors, metric, labels.reshape(1, n), train_mask.reshape(1, n))
    total, degree, means, msg = mean_call(over_dp(msg), anchors)
    means_a = lax.all_to_all(msg, "z", 0, 0, tiled=True)
    means_b = swap(means_a)
    own_ft = lax.dynamic_slice_in_dim(ft, shard[0] * OWN, OWN, 1)
    own_tags = lax.dynamic_slice_in_dim(tags, shard[0] * OWN, OWN, 1)
    embedding, up, down, part, loss = head_call(shard, metric, own_ft, means_a, means_b, cls_t, own_tags)
    blocks, cls = ring(up, down, part)
    blocks = [b for block in blocks for b in (block, swap(block))]
    msg, grads = mean_grad_call(shard, lb, blocks)
    msg = score_call(features, ft, rinv, excess, grads, am, anchors, metric, means, total, degree, loss, over_dp(msg))
    msg = jnp.concatenate([msg, cls.astype(bf16)], axis=0)
    grad_anchors, small = last_call(over_dp(msg))
    small = small + swap(small)
    small = lax.all_to_all(jnp.broadcast_to(small[None], (NZ,) + small.shape), "z", 0, 0, tiled=True)
    grad_metric, loss, grad_cls = finish_call(small, 1.0 / (4.0 * n * 16))
    return (embedding, loss.reshape(()), grad_cls.T, grad_anchors, grad_metric)


def solution(mesh):
    grid = Mesh(mesh.devices.reshape(4, 4, 8, 2), ("y", "x", "z", "c"))
    dp, sh = ("y", "x"), ("z", "c")
    return jax.shard_map(
        body,
        mesh=grid,
        in_specs=(P(dp, None), P(sh, None), P(), P(), P(dp), P(dp)),
        out_specs=(P(dp + sh, None), P(), P(), P(sh, None), P()),
        check_vma=False,
    )
```

```python
import jax
import jax.numpy as jnp
from jax import lax
from jax.experimental import pallas as pl
from jax.experimental.pallas import tpu as pltpu
from jax.sharding import Mesh
from jax.sharding import PartitionSpec as P

f32, bf16 = jnp.float32, jnp.bfloat16

threshold = 0.2
degree_floor = 0.25
F = 128
HEADS = 4
CLASSES = 172
CPAD = 256
OWN = 512
APD = 128
NZ = 8
MIB = 1024 * 1024

NN = ((1,), (0,))
NT = ((1,), (1,))
TN = ((0,), (0,))


def mm(a, b, dims, precision=None):
    return lax.dot_general(a, b, (dims, ((), ())), precision=precision, preferred_element_type=f32)


def params(mib=20):
    return pltpu.CompilerParams(vmem_limit_bytes=mib * MIB)


def vspec():
    return pl.BlockSpec(memory_space=pltpu.VMEM)


def column(row):
    return jnp.broadcast_to(row, (row.shape[1], row.shape[1])).T


def anchor_rows(anchors, metric, h):
    m = metric[h : h + 1, :]
    u = anchors * m
    r = lax.rsqrt(jnp.sum(u * u, axis=1, keepdims=True) + 1e-06)
    return u, r, m


def anchor_dirs(anchors, metric):
    rows = []
    for h in range(HEADS):
        u, r, _ = anchor_rows(anchors, metric, h)
        rows.append((u * (r * (1.0 / HEADS))).astype(bf16))
    return jnp.concatenate(rows, axis=1)


def node_dirs(ft, m_cols):
    dirs, norms = [], []
    for h in range(HEADS):
        u = ft * m_cols(h, ft.shape[1])
        r = lax.rsqrt(jnp.sum(u * u, axis=0, keepdims=True) + 1e-06)
        dirs.append((u * r).astype(bf16))
        norms.append(r)
    return jnp.concatenate(dirs, axis=0), jnp.concatenate(norms + norms, axis=0)


def wide_column(x, width):
    return jnp.concatenate([x] * (width // x.shape[1]), axis=1)


LINK_BLOCK = 2048
CHUNK = 256


def link_kernel(f_ref, a_ref, m_ref, lab_ref, mask_ref, ft_ref, rinv_ref, e_ref, lb_ref, tag_ref, am_ref, msg_ref, tot, raw, mc, ad):
    i = pl.program_id(0)

    @pl.when(i == 0)
    def _():
        anchors, metric = a_ref[...], m_ref[...]
        ad[...] = anchor_dirs(anchors, metric)
        for h in range(HEADS):
            u, r, m = anchor_rows(anchors, metric, h)
            am_ref[h * APD : (h + 1) * APD, :] = (u * r * m).astype(bf16)
            mc[h] = column(m)
        tot[...] = jnp.zeros_like(tot)
        raw[...] = jnp.zeros_like(raw)

    for j in range(LINK_BLOCK // CHUNK):
        cols = slice(j * CHUNK, (j + 1) * CHUNK)
        ft = f_ref[cols, :].astype(f32).T
        ft_ref[:, cols] = ft.astype(bf16)
        dirs, rinv = node_dirs(ft, lambda h, width: wide_column(mc[h], width))
        rinv_ref[:, cols] = rinv
        e = jnp.maximum(mm(ad[...], dirs, NN) - threshold, 0.0)
        link = e * e
        e_ref[:, cols] = e.astype(bf16)
        lb_ref[:, cols] = link.astype(bf16)
        raw[...] += sum(link[:, k * F : (k + 1) * F] for k in range(CHUNK // F))
    tot[...] += mm(lb_ref[...], f_ref[...], NN)
    tag_ref[...] = jnp.where(mask_ref[...] > 0, lab_ref[...], -1)

    @pl.when(i == pl.num_programs(0) - 1)
    def _():
        msg_ref[0:APD, :] = tot[...].astype(bf16)
        t = raw[...].T
        msg_ref[APD : APD + 16, :] = sum(t[16 * k : 16 * k + 16, :] for k in range(8)).astype(bf16)


def link_call(features, anchors, metric, labels, mask):
    n = features.shape[0]
    const = lambda i: (0, 0)
    wide = lambda rows: pl.BlockSpec((rows, LINK_BLOCK), lambda i: (0, i))
    return pl.pallas_call(
        link_kernel,
        grid=(n // LINK_BLOCK,),
        in_specs=[
            pl.BlockSpec((LINK_BLOCK, F), lambda i: (i, 0)),
            pl.BlockSpec((APD, F), const),
            pl.BlockSpec((HEADS, F), const),
            wide(1),
            wide(1),
        ],
        out_specs=[
            wide(F),
            wide(8),
            wide(APD),
            wide(APD),
            wide(1),
            pl.BlockSpec((HEADS * APD, F), const),
            pl.BlockSpec((APD + 16, F), const),
        ],
        out_shape=[
            jax.ShapeDtypeStruct((F, n), bf16),
            jax.ShapeDtypeStruct((8, n), f32),
            jax.ShapeDtypeStruct((APD, n), bf16),
            jax.ShapeDtypeStruct((APD, n), bf16),
            jax.ShapeDtypeStruct((1, n), jnp.int32),
            jax.ShapeDtypeStruct((HEADS * APD, F), bf16),
            jax.ShapeDtypeStruct((APD + 16, F), bf16),
        ],
        scratch_shapes=[
            pltpu.VMEM((APD, F), f32),
            pltpu.VMEM((APD, F), f32),
            pltpu.VMEM((HEADS, F, F), f32),
            pltpu.VMEM((APD, HEADS * F), bf16),
        ],
        compiler_params=params(60),
    )(features, anchors, metric, labels, mask)


def four(a, b, c, d):
    return (a[...].astype(f32) + b[...].astype(f32)) + (c[...].astype(f32) + d[...].astype(f32))


def mean_kernel(a, b, c, d, anchors_ref, total_ref, degree_ref, means_ref, msg_ref):
    s = four(a, b, c, d)
    total = s[0:APD, :]
    degree = column(jnp.sum(s[APD:, :], axis=0, keepdims=True) + degree_floor)
    total_ref[...] = total
    degree_ref[...] = degree
    means = (total / degree).astype(bf16)
    means_ref[...] = means
    anchors = anchors_ref[...].astype(bf16)
    for z in range(NZ):
        msg_ref[z, 0:APD, :] = means
        msg_ref[z, APD:, :] = anchors


def mean_call(parts, anchors):
    return pl.pallas_call(
        mean_kernel,
        in_specs=[vspec()] * 5,
        out_specs=[vspec()] * 4,
        out_shape=[
            jax.ShapeDtypeStruct((APD, F), f32),
            jax.ShapeDtypeStruct((APD, F), f32),
            jax.ShapeDtypeStruct((APD, F), bf16),
            jax.ShapeDtypeStruct((NZ, 2 * APD, F), bf16),
        ],
        compiler_params=params(),
    )(*parts, anchors)


HEAD_STEP = 4


def head_kernel(s_ref, m_ref, ft_ref, ma_ref, mb_ref, cls_ref, tag_ref, emb_ref, up_ref, down_ref, part_ref, loss_ref):
    metric = m_ref[...]
    dirs, _ = node_dirs(ft_ref[...].astype(f32), lambda h, width: wide_column(column(metric[h : h + 1, :]), width))

    def step(i, carry):
        field, raw = carry
        blocks = [ref[HEAD_STEP * i + k] for k in range(HEAD_STEP) for ref in (ma_ref, mb_ref)]
        ad = jnp.concatenate([anchor_dirs(b[APD:, :].astype(f32), metric) for b in blocks], axis=0)
        means = jnp.concatenate([b[0:APD, :] for b in blocks], axis=0)
        e = jnp.maximum(mm(ad, dirs, NN) - threshold, 0.0)
        link = e * e
        field = field + mm(means, link.astype(bf16), TN)
        raw = raw + sum(link[8 * k : 8 * k + 8, :] for k in range(link.shape[0] // 8))
        return field, raw

    field, raw = lax.fori_loop(0, NZ // HEAD_STEP, step, (jnp.zeros((F, OWN), f32), jnp.zeros((8, OWN), f32)))
    inv_degree = 1.0 / (jnp.sum(raw, axis=0, keepdims=True) + degree_floor)
    field = field * inv_degree
    emb_ref[...] = field.T.astype(bf16)
    highest = lax.Precision.HIGHEST
    cls_t = cls_ref[...]
    logits = mm(cls_t, field, NN, highest)
    ids = lax.broadcasted_iota(jnp.int32, (CPAD, OWN), 0)
    tag = tag_ref[...]
    residual = jnp.where(tag >= 0, logits - jnp.where(ids == tag, 1.0, 0.0), 0.0)
    loss_row = jnp.sum(residual * residual, axis=0, keepdims=True)
    loss_row = sum(loss_row[:, k * F : (k + 1) * F] for k in range(OWN // F))
    loss_ref[...] = jnp.concatenate([loss_row, jnp.zeros((7, F), f32)], axis=0)
    class_part = mm(residual, field, NT, highest)
    z = s_ref[0] // 2
    for k in range(NZ):
        part_ref[lax.rem(k - z + NZ, NZ)] = jnp.concatenate([class_part[32 * k + 8 * q : 32 * k + 8 * q + 8, :] for q in range(4)], axis=1)
    field_grad = mm(cls_t.T, residual, NN, highest)
    node_grads = (field_grad * inv_degree).astype(bf16)
    degree_grads = -jnp.sum(field_grad * field, axis=0, keepdims=True) * inv_degree
    for ref, k in ((up_ref, 4), (down_ref, 5)):
        ref[0:F, :] = node_grads
        ref[F : F + 16, :] = jnp.concatenate([degree_grads, jnp.zeros((7, OWN), f32), part_ref[k]], axis=0).astype(bf16)


def head_call(shard, *operands):
    return pl.pallas_call(
        head_kernel,
        in_specs=[pl.BlockSpec(memory_space=pltpu.SMEM)] + [vspec()] * len(operands),
        out_specs=[vspec()] * 5,
        out_shape=[
            jax.ShapeDtypeStruct((OWN, F), bf16),
            jax.ShapeDtypeStruct((F + 16, OWN), bf16),
            jax.ShapeDtypeStruct((F + 16, OWN), bf16),
            jax.ShapeDtypeStruct((NZ, 8, OWN), f32),
            jax.ShapeDtypeStruct((8, F), f32),
        ],
        compiler_params=params(),
    )(shard, *operands)


def mean_grad_kernel(s_ref, lb_ref, *refs):
    blocks, (msg_ref, all_ref) = refs[: 2 * NZ], refs[2 * NZ :]
    core = lax.rem(s_ref[0], 2)
    z = s_ref[0] // 2
    grads = jnp.zeros((APD, F), f32)
    for k, ref in enumerate(blocks):
        shard = 2 * lax.rem(z + k // 2, NZ) + (core if k % 2 == 0 else 1 - core)
        cols = pl.ds(pl.multiple_of(shard * OWN, OWN), OWN)
        all_ref[:, cols] = ref[...]
        grads = grads + mm(lb_ref[:, cols], ref[0:F, :], NT)
    msg_ref[...] = grads.astype(bf16)


def mean_grad_call(shard, lb, blocks):
    return pl.pallas_call(
        mean_grad_kernel,
        in_specs=[pl.BlockSpec(memory_space=pltpu.SMEM)] + [vspec()] * (1 + len(blocks)),
        out_specs=[vspec()] * 2,
        out_shape=[
            jax.ShapeDtypeStruct((APD, F), bf16),
            jax.ShapeDtypeStruct((F + 16, lb.shape[1]), bf16),
        ],
        compiler_params=params(),
    )(shard, lb, *blocks)


def score_kernel(
    f_ref, ft_ref, r_ref, e_ref, g_ref, am_ref, a_ref, m_ref, means_ref, total_ref, degree_ref, loss_ref,
    p0, p1, p2, p3, msg_ref, acc, vacc, lhs, adg, sgr
):
    i = pl.program_id(0)

    @pl.when(i == 0)
    def _():
        grads = four(p0, p1, p2, p3)
        inv = 1.0 / degree_ref[...]
        lhs[:, 0:F] = means_ref[...] * 0.5
        lhs[:, F:] = (grads * inv).astype(bf16) * 0.5
        dots = jnp.sum(grads * total_ref[...], axis=1, keepdims=True)
        adg[...] = (-2.0 / HEADS) * dots * (inv * inv)
        acc[...] = jnp.zeros_like(acc)
        vacc[...] = jnp.zeros_like(vacc)

    rows = []
    for j in range(SCORE_BLOCK // SCORE_CHUNK):
        cols = slice(j * SCORE_CHUNK, (j + 1) * SCORE_CHUNK)
        ft = ft_ref[:, cols]
        rinv = r_ref[:, cols]
        dg = g_ref[F : F + 16, cols].astype(f32)[0:1, :] * (2.0 / HEADS)
        link_grads = mm(lhs[...], jnp.concatenate([g_ref[0:F, cols], ft], axis=0), NN)
        sg = (link_grads + dg + wide_column(adg[...], SCORE_CHUNK)) * e_ref[:, cols].astype(f32)
        ws = []
        for h in range(HEADS):
            r = rinv[h : h + 1, :]
            sgr[h * APD : (h + 1) * APD, cols] = (sg * r).astype(bf16)
            prod = mm(am_ref[h * APD : (h + 1) * APD, :], ft, NN)
            ws.append(jnp.sum(sg * prod, axis=0, keepdims=True) * (r * r * r))
        w = jnp.concatenate(ws, axis=0)
        hi = w.astype(bf16).astype(f32)
        rows.append(jnp.concatenate([hi, w - hi], axis=0))
    v = jnp.concatenate(rows, axis=1).astype(bf16)
    fb = f_ref[...]
    acc[...] += mm(sgr[...], fb, NN)
    sq = fb.astype(f32)
    sq = sq * sq
    sq_hi = sq.astype(bf16)
    sq_lo = (sq - sq_hi.astype(f32)).astype(bf16)
    vacc[...] += mm(v, sq_hi, NN) + mm(v, sq_lo, NN)

    @pl.when(i == pl.num_programs(0) - 1)
    def _():
        anchors = a_ref[...]
        metric = m_ref[...]
        out = jnp.zeros((APD, F), f32)
        rows = []
        for h in range(HEADS):
            u, r, m = anchor_rows(anchors, metric, h)
            unit = u * r
            raw = acc[h * APD : (h + 1) * APD, :]
            grad = raw * m
            g = (grad - unit * jnp.sum(unit * grad, axis=1, keepdims=True)) * r
            out = out + g * m
            dirs = am_ref[h * APD : (h + 1) * APD, :].astype(f32)
            along = vacc[h : h + 1, :] + vacc[HEADS + h : HEADS + h + 1, :]
            row = jnp.sum(g * anchors, axis=0, keepdims=True)
            row = row + jnp.sum(dirs * raw, axis=0, keepdims=True) / m
            rows.append(row - m * along)
        msg_ref[0:APD, :] = out.astype(bf16)
        rows.append(loss_ref[0:1, :])
        rows.append(jnp.zeros((11, F), f32))
        msg_ref[APD : APD + 16, :] = jnp.concatenate(rows, axis=0).astype(bf16)


SCORE_BLOCK = 4096
SCORE_CHUNK = 256


def score_call(features, ft, rinv, excess, grads, am, anchors, metric, means, total, degree, loss, parts):
    n = features.shape[0]
    c2 = lambda i: (0, 0)
    whole = lambda x: pl.BlockSpec(x.shape, c2)
    wide = lambda x: pl.BlockSpec((x.shape[0], SCORE_BLOCK), lambda i: (0, i))
    return pl.pallas_call(
        score_kernel,
        grid=(n // SCORE_BLOCK,),
        in_specs=[pl.BlockSpec((SCORE_BLOCK, F), lambda i: (i, 0)), wide(ft), wide(rinv), wide(excess), wide(grads)]
        + [whole(x) for x in (am, anchors, metric, means, total, degree, loss, *parts)],
        out_specs=pl.BlockSpec((APD + 16, F), c2),
        out_shape=jax.ShapeDtypeStruct((APD + 16, F), bf16),
        scratch_shapes=[
            pltpu.VMEM((HEADS * APD, F), f32),
            pltpu.VMEM((8, F), f32),
            pltpu.VMEM((APD, 2 * F), bf16),
            pltpu.VMEM((APD, F), f32),
            pltpu.VMEM((HEADS * APD, SCORE_BLOCK), bf16),
        ],
        compiler_params=params(32),
    )(features, ft, rinv, excess, grads, am, anchors, metric, means, total, degree, loss, *parts)


def last_kernel(p0, p1, p2, p3, out_ref, small_ref):
    s = four(p0, p1, p2, p3)
    out_ref[...] = s[0:APD, :]
    small_ref[0:8, :] = s[APD : APD + 8, :]
    small_ref[8:40, :] = s[APD + 16 : APD + 48, :]


def last_call(parts):
    return pl.pallas_call(
        last_kernel,
        in_specs=[vspec()] * 4,
        out_specs=[vspec()] * 2,
        out_shape=[
            jax.ShapeDtypeStruct((APD, F), f32),
            jax.ShapeDtypeStruct((40, F), f32),
        ],
        compiler_params=params(),
    )(*parts)


def finish_kernel(scale, x_ref, metric_ref, loss_ref, cls_ref):
    s = x_ref[0, 0:8, :]
    for k in range(1, NZ):
        s = s + x_ref[k, 0:8, :]
    metric_ref[...] = s[0:HEADS, :]
    loss_ref[...] = jnp.sum(s[HEADS : HEADS + 1, :], axis=1, keepdims=True) * scale
    for z in range(NZ):
        rows = min(32, CLASSES - 32 * z)
        if rows > 0:
            cls_ref[32 * z : 32 * z + rows, :] = x_ref[z, 8 : 8 + rows, :]


def finish_call(x, scale):
    return pl.pallas_call(
        lambda *refs: finish_kernel(scale, *refs),
        in_specs=[vspec()],
        out_specs=[vspec()] * 3,
        out_shape=[
            jax.ShapeDtypeStruct((HEADS, F), f32),
            jax.ShapeDtypeStruct((1, 1), f32),
            jax.ShapeDtypeStruct((CLASSES, F), f32),
        ],
        compiler_params=params(),
    )(x)


def swap(x):
    return lax.ppermute(x, "c", [(0, 1), (1, 0)])


def shared(x, axis):
    others = [lax.ppermute(x, axis, [(i, i ^ k) for i in range(4)]) for k in (1, 2, 3)]
    return [x] + others


def sum4(parts):
    a, b, c, d = (p.astype(f32) for p in parts)
    return ((a + b) + (c + d)).astype(bf16)


def over_dp(x):
    return shared(sum4(shared(x, "x")), "y")


def ring(up, down, part):
    ups, downs = [(i, (i + 1) % NZ) for i in range(NZ)], [(i, (i - 1) % NZ) for i in range(NZ)]

    def add(x, k):
        total = x[F + 8 :].astype(f32) + part[k]
        return jnp.concatenate([x[: F + 8], total.astype(bf16)], axis=0)

    blocks = [up] + [None] * (NZ - 1)
    for k in range(1, 5):
        up = lax.ppermute(up, "z", ups)
        blocks[NZ - k] = up
        if k < 4:
            down = lax.ppermute(down, "z", downs)
            blocks[k] = down
            up = add(up, 4 - k)
        if k < 3:
            down = add(down, 5 + k)
    total = (up[F + 8 :].astype(f32) + down[F + 8 :].astype(f32)) + part[0]
    return blocks, jnp.concatenate([total[:, q * F : (q + 1) * F] for q in range(4)], axis=0)


def body(features, anchors, metric, classifier, labels, train_mask):
    n = features.shape[0]
    shard = (lax.axis_index("z") * 2 + lax.axis_index("c")).astype(jnp.int32).reshape(1)
    cls_t = jnp.pad(classifier.T, ((0, CPAD - CLASSES), (0, 0)))
    ft, rinv, excess, lb, tags, am, msg = link_call(features, anchors, metric, labels.reshape(1, n), train_mask.reshape(1, n))
    total, degree, means, msg = mean_call(over_dp(msg), anchors)
    means_a = lax.all_to_all(msg, "z", 0, 0, tiled=True)
    means_b = swap(means_a)
    own_ft = lax.dynamic_slice_in_dim(ft, shard[0] * OWN, OWN, 1)
    own_tags = lax.dynamic_slice_in_dim(tags, shard[0] * OWN, OWN, 1)
    embedding, up, down, part, loss = head_call(shard, metric, own_ft, means_a, means_b, cls_t, own_tags)
    blocks, cls = ring(up, down, part)
    blocks = [b for block in blocks for b in (block, swap(block))]
    msg, grads = mean_grad_call(shard, lb, blocks)
    msg = score_call(features, ft, rinv, excess, grads, am, anchors, metric, means, total, degree, loss, over_dp(msg))
    msg = jnp.concatenate([msg, cls.astype(bf16)], axis=0)
    grad_anchors, small = last_call(over_dp(msg))
    small = small + swap(small)
    small = lax.all_to_all(jnp.broadcast_to(small[None], (NZ,) + small.shape), "z", 0, 0, tiled=True)
    grad_metric, loss, grad_cls = finish_call(small, 1.0 / (4.0 * n * 16))
    return (embedding, loss.reshape(()), grad_cls.T, grad_anchors, grad_metric)


def solution(mesh):
    grid = Mesh(mesh.devices.reshape(4, 4, 8, 2), ("y", "x", "z", "c"))
    dp, sh = ("y", "x"), ("z", "c")
    return jax.shard_map(
        body,
        mesh=grid,
        in_specs=(P(dp, None), P(sh, None), P(), P(), P(dp), P(dp)),
        out_specs=(P(dp + sh, None), P(), P(), P(sh, None), P()),
        check_vma=False,
    )
```
